32 devices in a mesh: band: 2 (over x), gy: 4 (over y, core), gz: 4 (over z).
Axes of the slice: x: 2, y: 2, z: 4, core: 2. Of those that a mesh axis runs over, the one named last changes fastest.
Arguments:
- orbitals: bfloat16 [4, 128, 128, 256], P('band', 'gy', 'gz'), may hold values from -6 to 6
- potential: float32 [128, 128, 128], P(('gy', 'gz')), may hold values from -6 to 6
- cutoff_mask: int32 [128, 128, 128], P('gy', 'gz'), may hold values from 0 to 1, as said below
- channels: bfloat16 [4, 128, 128, 128], P(None, 'gy', 'gz'), may hold values from -0.125 to 0.125
- positions: float32 [8, 3], replicated, may hold values from 0 to 1
- proj_atom: int32 [32], replicated, may hold values from 0 to 7
- proj_chan: int32 [32], replicated, may hold values from 0 to 3
- coupling: float32 [32], replicated, may hold values from 0.5 to 2
- occupations: float32 [4], P('band'), may hold values from 0.25 to 0.75
Outputs:
- applied: bfloat16 [4, 128, 128, 256], P('band', 'gy', 'gz')
- density: float32 [128, 128, 128], P(('gy', 'gz'))
The draws below stay inside these ranges and needn't reach their ends.
Inputs may be any that keep to these rules, and one draw needn't show every extreme that they name: With s = f(ky)^2 + f(kz)^2 + f(kx)^2, cutoff_mask is 1 wherever s < 56^2 and 0 wherever s >= 128^2 / 4; in between each plane wave's value is its own.
All inputs are finite; a program needn't handle non-finite values.
Results may differ from the reference program's by a relative error of at most 0.018.
Values may be sent and summed in bfloat16 or wider, within the bound.
A program may use at most 128 MiB of HBM per device.

```python
import math
import jax
import jax.numpy as jnp
from jax import lax

NG = 128
BANDS = 4
CHAN = 4
ATOMS = 8
PROJ = 32


def draw_cutoff_mask(key, part):
    key = jax.random.fold_in(key, 7)
    inner = 7 * NG // 16 * (7 * NG // 16)
    outer = NG // 2 * (NG // 2)
    limits = jax.random.randint(key, (NG, NG, NG), inner, outer + 1, dtype=jnp.int32)
    grid_index = jnp.arange(NG, dtype=jnp.int32)
    wave_number = jnp.where(grid_index >= NG // 2, grid_index - NG, grid_index)
    squared = wave_number * wave_number
    total = squared[:, None, None] + squared[None, :, None] + squared[None, None, :]
    return (total < limits).astype(jnp.int32)


def set_ends(entries, rng, least, high):
    extent = entries.shape
    spot = [jax.random.randint(jax.random.fold_in(rng, axis), (), 0, extent[axis]) for axis in range(len(extent))]
    entries = entries.at[tuple(spot)].set(least)
    longest = extent.index(max(extent))
    spot[longest] = (spot[longest] + 1) % extent[longest]
    return entries.at[tuple(spot)].set(high)


def shard_levels(key, extent, cuts, smallest, largest):
    level, own = 1.0, jax.random.fold_in(key, 6)
    for position, blocks in cuts:
        steps = jnp.exp(jax.random.uniform(jax.random.fold_in(own, position), (blocks,), jnp.float32, smallest / len(cuts), largest / len(cuts)))
        level = level * jnp.repeat(steps, extent[position] // blocks).reshape([-1 if axis == position else 1 for axis in range(len(extent))])
    return level


def scatter_about(own_key, shape, width, most, pieces=(), held_as=jnp.bfloat16):
    entries = width * jax.random.normal(own_key, shape, jnp.float32)
    if pieces:
        entries = entries * shard_levels(own_key, shape, pieces, -0.22, 0.18)
    return jnp.clip(entries, -most, most).astype(held_as)


def setup_inputs(seed: int = 0) -> dict:
    arg_keys = jax.random.split(jax.random.key(seed), 10)
    orbitals = scatter_about(arg_keys[0], (BANDS, NG, NG, 2 * NG), 1.0, 6.0, ((0, 2), (1, 4), (2, 4)))
    potential = scatter_about(arg_keys[1], (NG, NG, NG), 1.0, 6.0, ((0, 16),), jnp.float32)
    cutoff_mask = draw_cutoff_mask(jax.random.fold_in(arg_keys[9], 71), 0)
    channels = scatter_about(arg_keys[3], (CHAN, NG, NG, NG), (1.0 / (2 * NG ** 3 * PROJ) ** 0.25), 0.125, ((1, 4), (2, 4)))
    positions = jnp.clip(jax.random.uniform(arg_keys[4], (ATOMS, 3), jnp.float32, 0.0, 1.0), 0.0, 1.0)
    proj_atom = set_ends(jax.random.randint(arg_keys[5], (PROJ,), 0, ATOMS), jax.random.fold_in(arg_keys[5], 1), 0, ATOMS - 1).astype(jnp.int32)
    proj_chan = set_ends(jax.random.randint(arg_keys[6], (PROJ,), 0, CHAN), jax.random.fold_in(arg_keys[6], 1), 0, CHAN - 1).astype(jnp.int32)
    coupling = jnp.clip(jnp.exp(jax.random.uniform(arg_keys[7], (PROJ,), jnp.float32, math.log(0.5), math.log(2.0))), 0.5, 2.0)
    occupations = jnp.clip(0.25 + 0.5 * jax.random.uniform(arg_keys[8], (BANDS,), jnp.float32) ** shard_levels(arg_keys[8], (BANDS,), ((0, 2),), -0.2, 0.2), 0.25, 0.75)
    return dict(orbitals=orbitals, potential=potential, cutoff_mask=cutoff_mask, channels=channels, positions=positions, proj_atom=proj_atom, proj_chan=proj_chan, coupling=coupling, occupations=occupations)


kinetic_scale = 1.0 / 1024.0

def dft_table(length, sign_value):
    grid_index = jnp.arange(length, dtype=jnp.int32)
    product = grid_index[:, None] * grid_index[None, :] % length
    phase_angle = 2.0 * math.pi / length * product.astype(jnp.float32)
    cosine_part = jnp.cos(phase_angle) / math.sqrt(length)
    sine_part = sign_value * jnp.sin(phase_angle) / math.sqrt(length)
    upper_rows = jnp.stack([cosine_part, -sine_part], axis=1)
    lower_rows = jnp.stack([sine_part, cosine_part], axis=1)
    return jnp.stack([upper_rows, lower_rows], axis=0).astype(jnp.bfloat16)

def frequencies(first_index, span, length):
    grid_index = first_index + jnp.arange(span, dtype=jnp.int32)
    return jnp.where(grid_index >= length // 2, grid_index - length, grid_index).astype(jnp.float32)

def axis_phase(coordinate, freq):
    phase_angle = 2.0 * math.pi * (coordinate[:, None] * freq[None, :])
    return (jnp.cos(phase_angle), jnp.sin(phase_angle))

def projector_parts(channels, positions, atom_ids, kind_ids, freq_y, freq_z, freq_x):
    atom_hot = (atom_ids[:, None] == jnp.arange(positions.shape[0], dtype=jnp.int32)[None, :]).astype(jnp.float32)
    located = jnp.dot(atom_hot, positions, precision=lax.Precision.HIGHEST)
    kind_hot = (kind_ids[:, None] == jnp.arange(channels.shape[0], dtype=jnp.int32)[None, :]).astype(jnp.bfloat16)
    radial = jnp.einsum('bc,cyzx->byzx', kind_hot, channels, preferred_element_type=jnp.float32)
    cos_y, sin_y = axis_phase(located[:, 1], freq_y)
    cos_z, sin_z = axis_phase(located[:, 2], freq_z)
    cos_x, sin_x = axis_phase(located[:, 0], freq_x)
    cos_yz = cos_y[:, :, None] * cos_z[:, None, :] - sin_y[:, :, None] * sin_z[:, None, :]
    sin_yz = sin_y[:, :, None] * cos_z[:, None, :] + cos_y[:, :, None] * sin_z[:, None, :]
    cosine = cos_yz[..., None] * cos_x[:, None, None, :] - sin_yz[..., None] * sin_x[:, None, None, :]
    sine = sin_yz[..., None] * cos_x[:, None, None, :] + cos_yz[..., None] * sin_x[:, None, None, :]
    real_beta = (radial * cosine).astype(jnp.bfloat16)
    imag_beta = (-(radial * sine)).astype(jnp.bfloat16)
    return (real_beta, imag_beta)

def reference(orbitals, potential, cutoff_mask, channels, positions, proj_atom, proj_chan, coupling, occupations):
    length = NG
    high = lax.Precision.HIGHEST
    inverse = dft_table(length, 1.0)
    forward = dft_table(length, -1.0)
    inv_x = jnp.transpose(inverse, (2, 3, 0, 1)).reshape(2 * length, 2, length).astype(jnp.float32)
    fwd_x = jnp.transpose(forward, (2, 3, 0, 1)).reshape(2, length, 2 * length).astype(jnp.float32)
    inv_f = inverse.astype(jnp.float32)
    fwd_f = forward.astype(jnp.float32)
    mask_full = jnp.concatenate([cutoff_mask, cutoff_mask], axis=2) != 0
    masked = jnp.where(mask_full[None], orbitals, jnp.zeros_like(orbitals))
    freq = frequencies(0, length, length)
    energy = kinetic_scale * 0.5 * (freq[:, None, None] ** 2 + freq[None, :, None] ** 2 + freq[None, None, :] ** 2)
    energy = jnp.concatenate([energy, energy], axis=2)
    block_size = min(PROJ, 16)
    block_count = PROJ // block_size
    atom_blocks = proj_atom.reshape(block_count, block_size)
    kind_blocks = proj_chan.reshape(block_count, block_size)
    real_orbs = masked[..., :length].astype(jnp.float32)
    imag_orbs = masked[..., length:].astype(jnp.float32)

    def intersection_step(state_in, indices):
        real_beta, imag_beta = projector_parts(channels, positions, indices[0], indices[1], freq, freq, freq)
        real_beta = real_beta.astype(jnp.float32)
        imag_beta = imag_beta.astype(jnp.float32)
        real_over = jnp.einsum('pyzx,nyzx->pn', real_beta, real_orbs) + jnp.einsum('pyzx,nyzx->pn', imag_beta, imag_orbs)
        imag_over = jnp.einsum('pyzx,nyzx->pn', real_beta, imag_orbs) - jnp.einsum('pyzx,nyzx->pn', imag_beta, real_orbs)
        return (state_in, jnp.stack([real_over, imag_over], axis=0))
    unused, intersections = lax.scan(intersection_step, jnp.zeros((), jnp.float32), (atom_blocks, kind_blocks))
    coefficients = intersections * coupling.reshape(block_count, 1, block_size, 1)
    coefficients = coefficients.astype(jnp.bfloat16)

    def apply_step(running, inputs):
        real_beta, imag_beta = projector_parts(channels, positions, inputs[0], inputs[1], freq, freq, freq)
        real_beta = real_beta.astype(jnp.float32)
        imag_beta = imag_beta.astype(jnp.float32)
        coef_real = inputs[2][0].astype(jnp.float32)
        coef_imag = inputs[2][1].astype(jnp.float32)
        real_sum = running[0] + jnp.einsum('pn,pyzx->nyzx', coef_real, real_beta) - jnp.einsum('pn,pyzx->nyzx', coef_imag, imag_beta)
        imag_sum = running[1] + jnp.einsum('pn,pyzx->nyzx', coef_imag, real_beta) + jnp.einsum('pn,pyzx->nyzx', coef_real, imag_beta)
        return ((real_sum, imag_sum), None)
    start_sums = (jnp.zeros(real_orbs.shape, jnp.float32), jnp.zeros(real_orbs.shape, jnp.float32))
    sums, unused_two = lax.scan(apply_step, start_sums, (atom_blocks, kind_blocks, coefficients))
    nonlocal_part = jnp.concatenate([sums[0], sums[1]], axis=3)

    def band_step(density, inputs):
        orbital, extra, weight = inputs
        spread = jnp.einsum('yzk,kcj->yzcj', orbital.astype(jnp.float32), inv_x, precision=high).astype(jnp.bfloat16)
        rotated = jnp.einsum('yzcj,ducy->uzdj', spread.astype(jnp.float32), inv_f, precision=high).astype(jnp.bfloat16)
        real_field = jnp.einsum('uzdj,fwdz->fjuw', rotated.astype(jnp.float32), inv_f, precision=high)
        density = density + weight * lax.optimization_barrier(jnp.sum(real_field * real_field, axis=0))
        scaled = (potential[None] * real_field).astype(jnp.bfloat16)
        back_z = jnp.einsum('fjuw,dzfw->uzdj', scaled.astype(jnp.float32), fwd_f, precision=high).astype(jnp.bfloat16)
        folded = jnp.einsum('uzdj,cydu->yzcj', back_z.astype(jnp.float32), fwd_f, precision=high).astype(jnp.bfloat16)
        local_g = jnp.einsum('yzcj,cjk->yzk', folded.astype(jnp.float32), fwd_x, precision=high)
        total = energy * orbital.astype(jnp.float32) + local_g + extra
        applied = jnp.where(mask_full, total, jnp.zeros_like(total)).astype(jnp.bfloat16)
        return (density, applied)
    density, applied = lax.scan(band_step, jnp.zeros((length, length, length), jnp.float32), (masked, nonlocal_part, occupations))
    return (applied, density)
```

```python
import functools
import math

import jax
import jax.numpy as jnp
import ml_dtypes
import numpy as np
from jax import lax
from jax.experimental import pallas as pl
from jax.experimental.pallas import tpu as pltpu
from jax.sharding import PartitionSpec as P

kinetic_scale = 1.0 / 1024.0
MESH = pl.DeviceIdType.MESH
F32 = jnp.float32
BF16 = jnp.bfloat16


def dot(a, b, dims):
    return lax.dot_general(a, b, (dims, ((), ())), preferred_element_type=F32)


def parts_of(length, sign_value):
    index = np.arange(length)
    angle = 2.0 * np.pi / length * (index[:, None] * index[None, :] % length)
    cosine = np.cos(angle) / math.sqrt(length)
    sine = sign_value * np.sin(angle) / math.sqrt(length)
    return cosine, sine


def tables(length, rows_z, parts_z):
    group = length // rows_z
    same = np.eye(group)
    out = []
    for sign in (1.0, -1.0):
        c, s = parts_of(length, sign)
        square = np.block([[c, -s], [s, c]])
        out.append(square)
    inv_sq, fwd_sq = out
    order = np.arange(2 * length).reshape(2, length // 8, 8).transpose(1, 0, 2).reshape(-1)
    inv_x = inv_sq[order]
    fwd_x = fwd_sq.T[order]
    c, s = parts_of(length, 1.0)
    z_in = [
        np.einsum("wqz,jk->qjzkw", t.reshape(length, parts_z, rows_z), same).reshape(
            parts_z * group * rows_z, group * length
        )
        for t in (c, s)
    ]
    c, s = parts_of(length, -1.0)
    z_out = [
        np.einsum("qzw,jk->jwqkz", t.reshape(parts_z, rows_z, length), same).reshape(
            group * length, parts_z * group * rows_z
        )
        for t in (c, s)
    ]
    made = (inv_x, np.concatenate(z_in, 1), inv_sq, fwd_sq, np.concatenate(z_out, 1), fwd_x)
    return [np.asarray(t, dtype=np.float32).astype(ml_dtypes.bfloat16) for t in made]


def kernel(
    sizes,
    orb_ref,
    mask_ref,
    pot_ref,
    chan_ref,
    pos_ref,
    posx_ref,
    match_ref,
    occ_ref,
    ix_ref,
    tz_ref,
    t2_ref,
    f2_ref,
    tb_ref,
    fx_ref,
    out_ref,
    dens_out_ref,
    masked,
    tx,
    rx,
    tx2,
    rx2,
    zs,
    dens,
    dens_rx,
    extra,
    phase,
    fold,
    over_tx,
    over_rx,
    send_sem,
    recv_sem,
    over_send,
    over_recv,
    dens_send,
    dens_recv,
):
    N, C, A, length, rows_y, rows_z, py, pz, bands = sizes
    L = 2 * C * N * A
    half = L // 2
    group = length // rows_z
    G = rows_y // group
    S = py * pz
    cols = rows_y * rows_z
    gy = lax.axis_index("gy")
    gz = lax.axis_index("gz")
    band = lax.axis_index("band")
    me = gy * pz + gz

    def peer(d):
        to = lax.rem(me + d, S)
        return to, {"gy": to // pz, "gz": lax.rem(to, pz)}

    barrier = pltpu.get_barrier_semaphore()

    def greet(d, c):
        pl.semaphore_signal(barrier, inc=1, device_id=peer(d)[1], device_id_type=MESH)
        return c

    def greet_band(d, c):
        pl.semaphore_signal(
            barrier, inc=1, device_id={"band": lax.rem(band + d, bands)}, device_id_type=MESH
        )
        return c

    lax.fori_loop(1, S, greet, 0)
    lax.fori_loop(1, bands, greet_band, 0)

    def block_copy(src, dst, step, n, to, place, slot):
        return pltpu.make_async_remote_copy(
            src_ref=src.at[to, n],
            dst_ref=dst.at[slot, n],
            send_sem=send_sem.at[step, n, to],
            recv_sem=recv_sem.at[step, n, slot],
            device_id=place,
            device_id_type=MESH,
        )

    def send_blocks(src, dst, step, n):
        def one(d, c):
            to, place = peer(d)
            block_copy(src, dst, step, n, to, place, me).start()
            return c

        lax.fori_loop(1, S, one, 0)
        dst[me, n] = src[me, n]

    def wait_blocks(src, dst, step, n):
        def one(d, c):
            frm, place = peer(d)
            block_copy(src, dst, step, n, frm, place, frm).wait_recv()
            return c

        lax.fori_loop(1, S, one, 0)

    def wait_sent(src, dst, step, n):
        def one(d, c):
            to, place = peer(d)
            block_copy(src, dst, step, n, to, place, me).wait_send()
            return c

        lax.fori_loop(1, S, one, 0)

    def x_group(n, g, c):
        rows = pl.ds(pl.multiple_of((n * G + g) * 128, 128), 128)
        keep = mask_ref[pl.ds(pl.multiple_of(g * 128, 128), 128), :] != 0
        keep = jnp.concatenate([keep.astype(F32)] * 2, axis=1) != 0
        block = jnp.where(keep, orb_ref[rows, :].astype(F32), 0.0).astype(BF16)
        masked[rows, :] = block
        made = dot(ix_ref[...], block, ((1,), (1,))).astype(BF16)
        tx[:, n, g] = made.reshape(S, 16, 128)
        return c

    for n in range(N):
        lax.fori_loop(0, G, functools.partial(x_group, n), 0)
        if n == 0:
            pl.semaphore_wait(barrier, S - 1 + bands - 1)
        send_blocks(tx, rx, 0, n)

    def centred(index):
        return jnp.where(index >= length // 2, index - length, index).astype(F32)

    def turn(amount):
        angle = (2.0 * math.pi) * (amount - jnp.round(amount))
        return jnp.cos(angle), jnp.sin(angle)

    fy = centred(lax.broadcasted_iota(jnp.int32, (rows_y, L), 0) + gy * rows_y)
    fz = centred(lax.broadcasted_iota(jnp.int32, (rows_z, L), 0) + gz * rows_z)
    fx = centred(lax.broadcasted_iota(jnp.int32, (L, length), 1))
    cy, sy = turn(fy * pos_ref[1:2, :])
    cz, sz = turn(fz * pos_ref[2:3, :])
    cx, sx = turn(fx * posx_ref[...])
    for y in range(rows_y):
        at = pl.ds(y * rows_z, rows_z)
        phase[0, at, :] = cy[y : y + 1] * cz - sy[y : y + 1] * sz
        phase[1, at, :] = sy[y : y + 1] * cz + cy[y : y + 1] * sz
    row = lax.broadcasted_iota(jnp.int32, (L, 2 * length), 0)
    pair = lax.rem(row, half) // A
    real_row = row < half
    cs = jnp.concatenate([cx, -sx], axis=1)
    sc = jnp.concatenate([sx, cx], axis=1)
    wave = jnp.where(real_row, cs, sc)
    for i in range(C * N):
        fold[i] = jnp.where(pair == i, wave, 0.0).astype(BF16)
    lane = lax.broadcasted_iota(jnp.int32, (1, L), 1)
    sign = jnp.where(lane < half, -1.0, 1.0)

    def over_group(g, total):
        at = pl.ds(pl.multiple_of(g * 128, 128), 128)
        found = jnp.zeros((128, L), F32)
        for c in range(C):
            profile = chan_ref[c, at, :]
            profile = jnp.concatenate([profile, profile], axis=1)
            for n in range(N):
                rows = pl.ds(pl.multiple_of(n * cols + g * 128, 128), 128)
                found = found + dot(profile * masked[rows, :], fold[c * N + n], ((1,), (1,)))
        swapped = pltpu.roll(found, half, 1)
        value = phase[0, at, :] * found + sign * (phase[1, at, :] * swapped)
        return total + jnp.sum(value, axis=0, keepdims=True)

    total = lax.fori_loop(0, G, over_group, jnp.zeros((1, L), F32))
    over_tx[...] = jnp.broadcast_to(total, (8, L))

    def over_copy(to, place, slot):
        return pltpu.make_async_remote_copy(
            src_ref=over_tx,
            dst_ref=over_rx.at[slot],
            send_sem=over_send.at[to],
            recv_sem=over_recv.at[slot],
            device_id=place,
            device_id_type=MESH,
        )

    def over_start(d, c):
        to, place = peer(d)
        over_copy(to, place, me).start()
        return c

    lax.fori_loop(1, S, over_start, 0)
    over_rx[me] = over_tx[...]

    for n in range(N):
        wait_blocks(tx, rx, 0, n)

        def z_in(q, c):
            lhs = jnp.concatenate(
                [rx[q * pz + k, n].reshape(G * 16, 128) for k in range(pz)], axis=1
            )
            made = dot(lhs, tz_ref[...], ((1,), (0,)))
            u = made[:, : group * length].reshape(G, 2, 8, group * length)
            v = made[:, group * length :].reshape(G, 2, 8, group * length)
            re = u[:, 0] - v[:, 1]
            im = v[:, 0] + u[:, 1]
            for g in range(G):
                for j in range(group):
                    at = pl.multiple_of((q * rows_y + g * group + j) * 16, 16)
                    zs[pl.ds(at, 8), :] = re[g, :, j * length : (j + 1) * length]
                    zs[pl.ds(at + 8, 8), :] = im[g, :, j * length : (j + 1) * length]
            return c

        lax.fori_loop(0, py, z_in, 0)
        for x in range(8):
            low = pl.ds(x, length, stride=16)
            high = pl.ds(x + 8, length, stride=16)
            both = jnp.concatenate([zs[low, :], zs[high, :]], axis=0).astype(BF16)
            field = dot(t2_ref[...], both, ((1,), (0,)))
            re, im = field[:length], field[length:]
            weight = occ_ref[n] * (re * re + im * im)
            if n == 0:
                dens[x] = weight
            else:
                dens[x] = dens[x] + weight
            pot = pot_ref[x]
            scaled = jnp.concatenate([pot * re, pot * im], axis=0).astype(BF16)
            back = dot(f2_ref[...], scaled, ((1,), (0,)))
            zs[low, :] = back[:length]
            zs[high, :] = back[length:]

        def z_out(q, c):
            at = pl.ds(pl.multiple_of(q * rows_y * 16, 512), rows_y * 16)
            block = zs[at, :].reshape(G, group, 16, length)
            lhs = jnp.concatenate(
                [block[:, j].reshape(G * 16, length) for j in range(group)], axis=1
            ).astype(BF16)
            made = dot(lhs, tb_ref[...], ((1,), (0,)))
            u = made[:, : pz * 128].reshape(G, 2, 8, pz * 128)
            v = made[:, pz * 128 :].reshape(G, 2, 8, pz * 128)
            re = u[:, 0] - v[:, 1]
            im = v[:, 0] + u[:, 1]
            joined = jnp.concatenate([re, im], axis=1).astype(BF16)
            for k in range(pz):
                tx2[q * pz + k, n] = joined[:, :, k * 128 : (k + 1) * 128]
            return c

        lax.fori_loop(0, py, z_out, 0)
        send_blocks(tx2, rx2, 1, n)

    dens_rx[band] = dens[...].astype(BF16)

    def dens_copy(d, slot):
        to = lax.rem(band + d, bands)
        return pltpu.make_async_remote_copy(
            src_ref=dens_rx.at[band],
            dst_ref=dens_rx.at[slot],
            send_sem=dens_send.at[to],
            recv_sem=dens_recv.at[slot],
            device_id={"band": to},
            device_id_type=MESH,
        )

    def dens_start(d, c):
        dens_copy(d, band).start()
        return c

    lax.fori_loop(1, bands, dens_start, 0)

    def over_wait(d, c):
        frm, place = peer(d)
        over_copy(frm, place, frm).wait_recv()
        return c

    lax.fori_loop(1, S, over_wait, 0)
    meet = over_rx[0]
    for s in range(1, S):
        meet = meet + over_rx[s]
    terms = (match_ref[...] * meet[0:1]).astype(BF16).astype(F32)
    coef = jnp.sum(terms, axis=0, keepdims=True)
    coef_swapped = pltpu.roll(jnp.broadcast_to(coef, (8, L)), half, 1)[0:1]

    def apply_group(g, c):
        at = pl.ds(pl.multiple_of(g * 128, 128), 128)
        lhs = phase[0, at, :] * coef - phase[1, at, :] * (sign * coef_swapped)
        lhs = lhs.astype(BF16)
        index = lax.broadcasted_iota(jnp.int32, (128, length), 0) + g * 128
        ky = centred(gy * rows_y + index // rows_z)
        kz = centred(gz * rows_z + lax.rem(index, rows_z))
        kx = centred(lax.broadcasted_iota(jnp.int32, (128, length), 1))
        energy = (kinetic_scale * 0.5) * (ky * ky + kz * kz + kx * kx)
        energy = jnp.concatenate([energy, energy], axis=1)
        sums = [None] * N
        for n in range(N):
            rows = pl.ds(pl.multiple_of(n * cols + g * 128, 128), 128)
            sums[n] = energy * masked[rows, :].astype(F32)
        for k in range(C):
            profile = chan_ref[k, at, :].astype(F32)
            profile = jnp.concatenate([profile, profile], axis=1)
            for n in range(N):
                sums[n] = sums[n] + profile * dot(lhs, fold[k * N + n], ((1,), (0,)))
        for n in range(N):
            rows = pl.ds(pl.multiple_of(n * cols + g * 128, 128), 128)
            extra[rows, :] = sums[n]
        return c

    lax.fori_loop(0, G, apply_group, 0)

    def dens_wait(d, c):
        dens_copy(d, lax.rem(band + d, bands)).wait_recv()
        return c

    lax.fori_loop(1, bands, dens_wait, 0)
    whole = dens_rx[0].astype(F32)
    for b in range(1, bands):
        whole = whole + dens_rx[b].astype(F32)
    dens_out_ref[...] = whole

    for n in range(N):
        wait_blocks(tx2, rx2, 1, n)

        def finish(g, c):
            rows = pl.ds(pl.multiple_of((n * G + g) * 128, 128), 128)
            keep = mask_ref[pl.ds(pl.multiple_of(g * 128, 128), 128), :] != 0
            keep = jnp.concatenate([keep.astype(F32)] * 2, axis=1) != 0
            block = rx2[:, n, g].reshape(S * 16, 128)
            local = dot(block, fx_ref[...], ((0,), (0,)))
            out_ref[rows, :] = jnp.where(keep, local + extra[rows, :], 0.0).astype(BF16)
            return c

        lax.fori_loop(0, G, finish, 0)

    for n in range(N):
        wait_sent(tx, rx, 0, n)
        wait_sent(tx2, rx2, 1, n)

    def over_done(d, c):
        to, place = peer(d)
        over_copy(to, place, me).wait_send()
        return c

    lax.fori_loop(1, S, over_done, 0)

    def dens_done(d, c):
        dens_copy(d, band).wait_send()
        return c

    lax.fori_loop(1, bands, dens_done, 0)


def shards(
    orbitals,
    potential,
    cutoff_mask,
    channels,
    positions,
    proj_atom,
    proj_chan,
    coupling,
    occupations,
):
    N, rows_y, rows_z, wide = orbitals.shape
    length = wide // 2
    C = channels.shape[0]
    A = positions.shape[0]
    py, pz, bands = lax.axis_size("gy"), lax.axis_size("gz"), lax.axis_size("band")
    S = py * pz
    L = 2 * C * N * A
    G = rows_y * rows_z // 128
    cols = rows_y * rows_z
    made = [jnp.asarray(t) for t in tables(length, rows_z, pz)]
    lanes = jnp.arange(L, dtype=jnp.int32)
    lane_chan = lanes % (L // 2) // (N * A)
    lane_atom = lanes % A
    same = (proj_chan[:, None] == lane_chan[None]) & (proj_atom[:, None] == lane_atom[None])
    match = jnp.where(same, coupling[:, None], 0.0)
    tiled = jnp.tile(positions, (L // A, 1))
    vmem = pl.BlockSpec(memory_space=pltpu.VMEM)
    smem = pl.BlockSpec(memory_space=pltpu.SMEM)
    sizes = (N, C, A, length, rows_y, rows_z, py, pz, bands)
    planes = (S, N, G, 16, 128)
    applied, density = pl.pallas_call(
        functools.partial(kernel, sizes),
        out_shape=(
            jax.ShapeDtypeStruct((N * cols, wide), BF16),
            jax.ShapeDtypeStruct(potential.shape, F32),
        ),
        in_specs=[vmem] * 7 + [smem] + [vmem] * 6,
        out_specs=(vmem, vmem),
        scratch_shapes=[
            pltpu.VMEM((N * cols, wide), BF16),
            pltpu.VMEM(planes, BF16),
            pltpu.VMEM(planes, BF16),
            pltpu.VMEM(planes, BF16),
            pltpu.VMEM(planes, BF16),
            pltpu.VMEM((length * 16, length), F32),
            pltpu.VMEM(potential.shape, F32),
            pltpu.VMEM((bands,) + potential.shape, BF16),
            pltpu.VMEM((N * cols, wide), F32),
            pltpu.VMEM((2, cols, L), F32),
            pltpu.VMEM((C * N, L, wide), BF16),
            pltpu.VMEM((8, L), F32),
            pltpu.VMEM((S, 8, L), F32),
            pltpu.SemaphoreType.DMA((2, N, S)),
            pltpu.SemaphoreType.DMA((2, N, S)),
            pltpu.SemaphoreType.DMA((S,)),
            pltpu.SemaphoreType.DMA((S,)),
            pltpu.SemaphoreType.DMA((bands,)),
            pltpu.SemaphoreType.DMA((bands,)),
        ],
        compiler_params=pltpu.CompilerParams(
            collective_id=0, has_side_effects=True, vmem_limit_bytes=56 * 1024 * 1024
        ),
    )(
        orbitals.reshape(N * cols, wide),
        cutoff_mask.reshape(cols, length),
        potential,
        channels.reshape(C, cols, length),
        tiled.T,
        tiled[:, 0:1],
        match,
        occupations,
        *made,
    )
    return (applied.reshape(orbitals.shape), density)


def solution(mesh):
    placed = (
        P("band", "gy", "gz", None),
        P(("gy", "gz"), None, None),
        P("gy", "gz", None),
        P(None, "gy", "gz", None),
        P(),
        P(),
        P(),
        P(),
        P("band"),
    )
    return jax.shard_map(
        shards,
        mesh=mesh,
        in_specs=placed,
        out_specs=(P("band", "gy", "gz", None), P(("gy", "gz"), None, None)),
        check_vma=False,
    )
```

```python
import functools
import math

import jax
import jax.numpy as jnp
import ml_dtypes
import numpy as np
from jax import lax
from jax.experimental import pallas as pl
from jax.experimental.pallas import tpu as pltpu
from jax.sharding import PartitionSpec as P

kinetic_scale = 1.0 / 1024.0
MESH = pl.DeviceIdType.MESH
F32 = jnp.float32
BF16 = jnp.bfloat16


def dot(a, b, dims):
    return lax.dot_general(a, b, (dims, ((), ())), preferred_element_type=F32)


def parts_of(length, sign_value):
    index = np.arange(length)
    angle = 2.0 * np.pi / length * (index[:, None] * index[None, :] % length)
    cosine = np.cos(angle) / math.sqrt(length)
    sine = sign_value * np.sin(angle) / math.sqrt(length)
    return cosine, sine


def tables(length, rows_z, parts_z):
    group = length // rows_z
    same = np.eye(group)
    out = []
    for sign in (1.0, -1.0):
        c, s = parts_of(length, sign)
        square = np.block([[c, -s], [s, c]])
        out.append(square)
    inv_sq, fwd_sq = out
    order = np.arange(2 * length).reshape(2, length // 8, 8).transpose(1, 0, 2).reshape(-1)
    inv_x = inv_sq[order]
    fwd_x = fwd_sq.T[order]
    c, s = parts_of(length, 1.0)
    z_in = [
        np.einsum("wqz,jk->qjzkw", t.reshape(length, parts_z, rows_z), same).reshape(
            parts_z * group * rows_z, group * length
        )
        for t in (c, s)
    ]
    c, s = parts_of(length, -1.0)
    z_out = [
        np.einsum("qzw,jk->jwqkz", t.reshape(parts_z, rows_z, length), same).reshape(
            group * length, parts_z * group * rows_z
        )
        for t in (c, s)
    ]
    made = (inv_x, np.concatenate(z_in, 1), inv_sq, fwd_sq, np.concatenate(z_out, 1), fwd_x)
    return [np.asarray(t, dtype=np.float32).astype(ml_dtypes.bfloat16) for t in made]


def kernel(
    sizes,
    pos_ref,
    atom_ref,
    kind_ref,
    coup_ref,
    occ_ref,
    orb_hbm,
    mask_hbm,
    ix_hbm,
    chan_hbm,
    tz_hbm,
    t2_hbm,
    pot_hbm,
    f2_hbm,
    tb_hbm,
    fx_hbm,
    out_hbm,
    dens_hbm,
    orb_ref,
    mask_ref,
    ix_ref,
    chan_ref,
    tz_ref,
    t2_ref,
    pot_ref,
    f2_ref,
    tb_ref,
    fx_ref,
    out_ref,
    dens_out_ref,
    in_sem,
    out_sem,
    masked,
    tx,
    rx,
    tx2,
    rx2,
    zs,
    dens,
    dens_rx,
    extra,
    phase,
    fold,
    over_tx,
    over_rx,
    send_sem,
    recv_sem,
    over_send,
    over_recv,
    dens_send,
    dens_recv,
):
    N, C, A, length, rows_y, rows_z, py, pz, bands = sizes
    L = 2 * C * N * A
    half = L // 2
    group = length // rows_z
    G = rows_y // group
    S = py * pz
    cols = rows_y * rows_z
    gy = lax.axis_index("gy")
    gz = lax.axis_index("gz")
    band = lax.axis_index("band")
    me = gy * pz + gz

    half_rows = cols
    moves = [
        pltpu.make_async_copy(
            orb_hbm.at[pl.ds(n * half_rows, half_rows)],
            orb_ref.at[pl.ds(n * half_rows, half_rows)],
            in_sem.at[n],
        )
        for n in range(N)
    ]
    held = (
        (ix_hbm, ix_ref),
        (mask_hbm, mask_ref),
        (chan_hbm, chan_ref),
        (tz_hbm, tz_ref),
        (t2_hbm, t2_ref),
        (pot_hbm, pot_ref),
        (f2_hbm, f2_ref),
        (tb_hbm, tb_ref),
        (fx_hbm, fx_ref),
    )
    loads = [pltpu.make_async_copy(a, b, in_sem.at[N + i]) for i, (a, b) in enumerate(held)]
    for move in loads[:2] + moves + loads[2:]:
        move.start()

    def peer(d):
        to = lax.rem(me + d, S)
        return to, {"gy": to // pz, "gz": lax.rem(to, pz)}

    def place_of(to_y, to_z):
        return to_y * pz + to_z, {"gy": to_y, "gz": to_z}

    if pz == 4:
        far = [lax.rem(gz + 2, pz), 3 - gz, gz + 1 - 2 * lax.rem(gz, 2)]
    else:
        far = [lax.rem(gz + k, pz) for k in range(1, pz)]

    barrier = pltpu.get_barrier_semaphore()

    def greet(d, c):
        pl.semaphore_signal(barrier, inc=1, device_id=peer(d)[1], device_id_type=MESH)
        return c

    def greet_band(d, c):
        pl.semaphore_signal(
            barrier, inc=1, device_id={"band": lax.rem(band + d, bands)}, device_id_type=MESH
        )
        return c

    lax.fori_loop(1, S, greet, 0)
    lax.fori_loop(1, bands, greet_band, 0)

    def block_copy(src, dst, step, n, to, place, slot):
        return pltpu.make_async_remote_copy(
            src_ref=src.at[to, n],
            dst_ref=dst.at[slot, n],
            send_sem=send_sem.at[step, n, to],
            recv_sem=recv_sem.at[step, n, slot],
            device_id=place,
            device_id_type=MESH,
        )

    def send_blocks(src, dst, step, n):
        for to_z in far + [gz]:

            def one(d, c):
                to, place = place_of(lax.rem(gy + d, py), to_z)
                block_copy(src, dst, step, n, to, place, me).start()
                return c

            lax.fori_loop(1 if to_z is gz else 0, py, one, 0)
        dst[me, n] = src[me, n]

    def wait_blocks(src, dst, step, n):
        def one(d, c):
            frm, place = peer(d)
            block_copy(src, dst, step, n, frm, place, frm).wait_recv()
            return c

        lax.fori_loop(1, S, one, 0)

    def wait_sent(src, dst, step, n):
        def one(d, c):
            to, place = peer(d)
            block_copy(src, dst, step, n, to, place, me).wait_send()
            return c

        lax.fori_loop(1, S, one, 0)

    def x_group(n, g, c):
        rows = pl.ds(pl.multiple_of((n * G + g) * 128, 128), 128)
        keep = mask_ref[pl.ds(pl.multiple_of(g * 128, 128), 128), :] != 0
        keep = jnp.concatenate([keep.astype(F32)] * 2, axis=1) != 0
        block = jnp.where(keep, orb_ref[rows, :].astype(F32), 0.0).astype(BF16)
        masked[rows, :] = block
        made = dot(ix_ref[...], block, ((1,), (1,))).astype(BF16)
        tx[:, n, g] = made.reshape(S, 16, 128)
        return c

    loads[0].wait()
    loads[1].wait()
    for n in range(N):
        moves[n].wait()
        lax.fori_loop(0, G, functools.partial(x_group, n), 0)
        if n == 0:
            pl.semaphore_wait(barrier, S - 1 + bands - 1)
        send_blocks(tx, rx, 0, n)

    def centred(index):
        return jnp.where(index >= length // 2, index - length, index).astype(F32)

    def turn(amount):
        angle = (2.0 * math.pi) * (amount - jnp.round(amount))
        return jnp.cos(angle), jnp.sin(angle)

    fy = centred(lax.broadcasted_iota(jnp.int32, (rows_y, L), 0) + gy * rows_y)
    fz = centred(lax.broadcasted_iota(jnp.int32, (rows_z, L), 0) + gz * rows_z)
    fx = centred(lax.broadcasted_iota(jnp.int32, (L, length), 1))
    lane = lax.broadcasted_iota(jnp.int32, (1, L), 1)
    lane_atom = lax.rem(lane, A)
    lane_chan = lax.rem(lane, half) // (N * A)
    row_atom = lax.rem(lax.broadcasted_iota(jnp.int32, (L, length), 0), A)
    at_x = jnp.zeros((L, length), F32)
    at_y = jnp.zeros((1, L), F32)
    at_z = jnp.zeros((1, L), F32)
    for a in range(A):
        at_x = jnp.where(row_atom == a, pos_ref[0, a], at_x)
        at_y = jnp.where(lane_atom == a, pos_ref[1, a], at_y)
        at_z = jnp.where(lane_atom == a, pos_ref[2, a], at_z)
    cy, sy = turn(fy * at_y)
    cz, sz = turn(fz * at_z)
    cx, sx = turn(fx * at_x)
    for y in range(rows_y):
        at = pl.ds(y * rows_z, rows_z)
        phase[0, at, :] = cy[y : y + 1] * cz - sy[y : y + 1] * sz
        phase[1, at, :] = sy[y : y + 1] * cz + cy[y : y + 1] * sz
    row = lax.broadcasted_iota(jnp.int32, (L, 2 * length), 0)
    pair = lax.rem(row, half) // A
    real_row = row < half
    cs = jnp.concatenate([cx, -sx], axis=1)
    sc = jnp.concatenate([sx, cx], axis=1)
    wave = jnp.where(real_row, cs, sc)
    for i in range(C * N):
        fold[i] = jnp.where(pair == i, wave, 0.0).astype(BF16)
    sign = jnp.where(lane < half, -1.0, 1.0)

    loads[2].wait()

    def over_group(g, total):
        at = pl.ds(pl.multiple_of(g * 128, 128), 128)
        found = jnp.zeros((128, L), F32)
        for c in range(C):
            profile = chan_ref[c, at, :]
            profile = jnp.concatenate([profile, profile], axis=1)
            for n in range(N):
                rows = pl.ds(pl.multiple_of(n * cols + g * 128, 128), 128)
                found = found + dot(profile * masked[rows, :], fold[c * N + n], ((1,), (1,)))
        swapped = pltpu.roll(found, half, 1)
        value = phase[0, at, :] * found + sign * (phase[1, at, :] * swapped)
        return total + jnp.sum(value, axis=0, keepdims=True)

    total = lax.fori_loop(0, G, over_group, jnp.zeros((1, L), F32))
    over_tx[...] = jnp.broadcast_to(total, (8, L))

    def over_copy(to, place, slot):
        return pltpu.make_async_remote_copy(
            src_ref=over_tx,
            dst_ref=over_rx.at[slot],
            send_sem=over_send.at[to],
            recv_sem=over_recv.at[slot],
            device_id=place,
            device_id_type=MESH,
        )

    def over_start(d, c):
        to, place = peer(d)
        over_copy(to, place, me).start()
        return c

    lax.fori_loop(1, S, over_start, 0)
    over_rx[me] = over_tx[...]

    for move in loads[3:]:
        move.wait()
    for n in range(N):
        wait_blocks(tx, rx, 0, n)

        def z_in(q, c):
            lhs = jnp.concatenate(
                [rx[q * pz + k, n].reshape(G * 16, 128) for k in range(pz)], axis=1
            )
            made = dot(lhs, tz_ref[...], ((1,), (0,)))
            u = made[:, : group * length].reshape(G, 2, 8, group * length)
            v = made[:, group * length :].reshape(G, 2, 8, group * length)
            re = u[:, 0] - v[:, 1]
            im = v[:, 0] + u[:, 1]
            for g in range(G):
                for j in range(group):
                    at = pl.multiple_of((q * rows_y + g * group + j) * 16, 16)
                    zs[pl.ds(at, 8), :] = re[g, :, j * length : (j + 1) * length]
                    zs[pl.ds(at + 8, 8), :] = im[g, :, j * length : (j + 1) * length]
            return c

        lax.fori_loop(0, py, z_in, 0)
        for x in range(8):
            low = pl.ds(x, length, stride=16)
            high = pl.ds(x + 8, length, stride=16)
            both = jnp.concatenate([zs[low, :], zs[high, :]], axis=0).astype(BF16)
            field = dot(t2_ref[...], both, ((1,), (0,)))
            re, im = field[:length], field[length:]
            weight = occ_ref[n] * (re * re + im * im)
            if n == 0:
                dens[x] = weight
            else:
                dens[x] = dens[x] + weight
            pot = pot_ref[x]
            scaled = jnp.concatenate([pot * re, pot * im], axis=0).astype(BF16)
            back = dot(f2_ref[...], scaled, ((1,), (0,)))
            zs[low, :] = back[:length]
            zs[high, :] = back[length:]

        def z_out(q, c):
            at = pl.ds(pl.multiple_of(q * rows_y * 16, 512), rows_y * 16)
            block = zs[at, :].reshape(G, group, 16, length)
            lhs = jnp.concatenate(
                [block[:, j].reshape(G * 16, length) for j in range(group)], axis=1
            ).astype(BF16)
            made = dot(lhs, tb_ref[...], ((1,), (0,)))
            u = made[:, : pz * 128].reshape(G, 2, 8, pz * 128)
            v = made[:, pz * 128 :].reshape(G, 2, 8, pz * 128)
            re = u[:, 0] - v[:, 1]
            im = v[:, 0] + u[:, 1]
            joined = jnp.concatenate([re, im], axis=1).astype(BF16)
            for k in range(pz):
                tx2[q * pz + k, n] = joined[:, :, k * 128 : (k + 1) * 128]
            return c

        lax.fori_loop(0, py, z_out, 0)
        send_blocks(tx2, rx2, 1, n)

    dens_rx[band] = dens[...].astype(BF16)

    def dens_copy(d, slot):
        to = lax.rem(band + d, bands)
        return pltpu.make_async_remote_copy(
            src_ref=dens_rx.at[band],
            dst_ref=dens_rx.at[slot],
            send_sem=dens_send.at[to],
            recv_sem=dens_recv.at[slot],
            device_id={"band": to},
            device_id_type=MESH,
        )

    def dens_start(d, c):
        dens_copy(d, band).start()
        return c

    lax.fori_loop(1, bands, dens_start, 0)

    def over_wait(d, c):
        frm, place = peer(d)
        over_copy(frm, place, frm).wait_recv()
        return c

    lax.fori_loop(1, S, over_wait, 0)
    meet = over_rx[0]
    for s in range(1, S):
        meet = meet + over_rx[s]
    meet = meet[0:1]
    coef = jnp.zeros((1, L), F32)
    for p in range(coup_ref.shape[0]):
        hit = (lane_chan == kind_ref[p]) & (lane_atom == atom_ref[p])
        coef = coef + jnp.where(hit, (coup_ref[p] * meet).astype(BF16).astype(F32), 0.0)
    coef_swapped = pltpu.roll(jnp.broadcast_to(coef, (8, L)), half, 1)[0:1]

    def apply_group(g, c):
        at = pl.ds(pl.multiple_of(g * 128, 128), 128)
        lhs = phase[0, at, :] * coef - phase[1, at, :] * (sign * coef_swapped)
        lhs = lhs.astype(BF16)
        index = lax.broadcasted_iota(jnp.int32, (128, length), 0) + g * 128
        ky = centred(gy * rows_y + index // rows_z)
        kz = centred(gz * rows_z + lax.rem(index, rows_z))
        kx = centred(lax.broadcasted_iota(jnp.int32, (128, length), 1))
        energy = (kinetic_scale * 0.5) * (ky * ky + kz * kz + kx * kx)
        energy = jnp.concatenate([energy, energy], axis=1)
        sums = [None] * N
        for n in range(N):
            rows = pl.ds(pl.multiple_of(n * cols + g * 128, 128), 128)
            sums[n] = energy * masked[rows, :].astype(F32)
        for k in range(C):
            profile = chan_ref[k, at, :].astype(F32)
            profile = jnp.concatenate([profile, profile], axis=1)
            for n in range(N):
                sums[n] = sums[n] + profile * dot(lhs, fold[k * N + n], ((1,), (0,)))
        for n in range(N):
            rows = pl.ds(pl.multiple_of(n * cols + g * 128, 128), 128)
            extra[rows, :] = sums[n]
        return c

    lax.fori_loop(0, G, apply_group, 0)

    def dens_wait(d, c):
        dens_copy(d, lax.rem(band + d, bands)).wait_recv()
        return c

    lax.fori_loop(1, bands, dens_wait, 0)
    whole = dens_rx[0].astype(F32)
    for b in range(1, bands):
        whole = whole + dens_rx[b].astype(F32)
    dens_out_ref[...] = whole
    dens_move = pltpu.make_async_copy(dens_out_ref, dens_hbm, out_sem.at[N])
    dens_move.start()

    leaves = []
    for n in range(N):
        wait_blocks(tx2, rx2, 1, n)

        def finish(g, c):
            rows = pl.ds(pl.multiple_of((n * G + g) * 128, 128), 128)
            keep = mask_ref[pl.ds(pl.multiple_of(g * 128, 128), 128), :] != 0
            keep = jnp.concatenate([keep.astype(F32)] * 2, axis=1) != 0
            block = rx2[:, n, g].reshape(S * 16, 128)
            local = dot(block, fx_ref[...], ((0,), (0,)))
            out_ref[rows, :] = jnp.where(keep, local + extra[rows, :], 0.0).astype(BF16)
            return c

        lax.fori_loop(0, G, finish, 0)
        span = pl.ds(n * half_rows, half_rows)
        leave = pltpu.make_async_copy(out_ref.at[span], out_hbm.at[span], out_sem.at[n])
        leave.start()
        leaves.append(leave)

    for n in range(N):
        wait_sent(tx, rx, 0, n)
        wait_sent(tx2, rx2, 1, n)

    def over_done(d, c):
        to, place = peer(d)
        over_copy(to, place, me).wait_send()
        return c

    lax.fori_loop(1, S, over_done, 0)

    def dens_done(d, c):
        dens_copy(d, band).wait_send()
        return c

    lax.fori_loop(1, bands, dens_done, 0)
    dens_move.wait()
    for leave in leaves:
        leave.wait()


def hand_on(pieces, *refs):
    count = len(refs) // 2
    sem = refs[-1]
    moves = []
    for i in range(count):
        src, dst = refs[i], refs[count + i]
        rows = src.shape[0] // pieces
        for k in range(pieces):
            span = pl.ds(k * rows, rows)
            moves.append(pltpu.make_async_copy(src.at[span], dst.at[span], sem.at[i, k]))
    for move in moves:
        move.start()
    for move in moves:
        move.wait()


def shards(
    orbitals,
    potential,
    cutoff_mask,
    channels,
    positions,
    proj_atom,
    proj_chan,
    coupling,
    occupations,
):
    N, rows_y, rows_z, wide = orbitals.shape
    length = wide // 2
    C = channels.shape[0]
    A = positions.shape[0]
    py, pz, bands = lax.axis_size("gy"), lax.axis_size("gz"), lax.axis_size("band")
    S = py * pz
    L = 2 * C * N * A
    G = rows_y * rows_z // 128
    cols = rows_y * rows_z
    ix, tz, t2, f2, tb, fx = [jnp.asarray(t) for t in tables(length, rows_z, pz)]
    hbm = pl.BlockSpec(memory_space=pl.ANY)
    smem = pl.BlockSpec(memory_space=pltpu.SMEM)
    sizes = (N, C, A, length, rows_y, rows_z, py, pz, bands)
    planes = (S, N, G, 16, 128)
    applied, density = pl.pallas_call(
        functools.partial(kernel, sizes),
        out_shape=(
            jax.ShapeDtypeStruct((N * cols, wide), BF16),
            jax.ShapeDtypeStruct(potential.shape, F32),
        ),
        in_specs=[smem] * 5 + [hbm] * 10,
        out_specs=(hbm, hbm),
        scratch_shapes=[
            pltpu.VMEM((N * cols, wide), BF16),
            pltpu.VMEM((cols, length), jnp.int32),
            pltpu.VMEM(ix.shape, BF16),
            pltpu.VMEM((C, cols, length), BF16),
            pltpu.VMEM(tz.shape, BF16),
            pltpu.VMEM(t2.shape, BF16),
            pltpu.VMEM(potential.shape, F32),
            pltpu.VMEM(f2.shape, BF16),
            pltpu.VMEM(tb.shape, BF16),
            pltpu.VMEM(fx.shape, BF16),
            pltpu.VMEM((N * cols, wide), BF16),
            pltpu.VMEM(potential.shape, F32),
            pltpu.SemaphoreType.DMA((N + 9,)),
            pltpu.SemaphoreType.DMA((N + 1,)),
            pltpu.VMEM((N * cols, wide), BF16),
            pltpu.VMEM(planes, BF16),
            pltpu.VMEM(planes, BF16),
            pltpu.VMEM(planes, BF16),
            pltpu.VMEM(planes, BF16),
            pltpu.VMEM((length * 16, length), F32),
            pltpu.VMEM(potential.shape, F32),
            pltpu.VMEM((bands,) + potential.shape, BF16),
            pltpu.VMEM((N * cols, wide), F32),
            pltpu.VMEM((2, cols, L), F32),
            pltpu.VMEM((C * N, L, wide), BF16),
            pltpu.VMEM((8, L), F32),
            pltpu.VMEM((S, 8, L), F32),
            pltpu.SemaphoreType.DMA((2, N, S)),
            pltpu.SemaphoreType.DMA((2, N, S)),
            pltpu.SemaphoreType.DMA((S,)),
            pltpu.SemaphoreType.DMA((S,)),
            pltpu.SemaphoreType.DMA((bands,)),
            pltpu.SemaphoreType.DMA((bands,)),
        ],
        compiler_params=pltpu.CompilerParams(
            collective_id=0, has_side_effects=True, vmem_limit_bytes=56 * 1024 * 1024
        ),
    )(
        positions.T,
        proj_atom,
        proj_chan,
        coupling,
        occupations,
        orbitals.reshape(N * cols, wide),
        cutoff_mask.reshape(cols, length),
        ix,
        channels.reshape(C, cols, length),
        tz,
        t2,
        potential,
        f2,
        tb,
        fx,
    )
    pieces = 4
    applied, density = pl.pallas_call(
        functools.partial(hand_on, pieces),
        out_shape=(
            jax.ShapeDtypeStruct((N * cols, wide), BF16),
            jax.ShapeDtypeStruct(potential.shape, F32),
        ),
        in_specs=[hbm] * 2,
        out_specs=(hbm, hbm),
        scratch_shapes=[pltpu.SemaphoreType.DMA((2, pieces))],
    )(applied, density)
    return (applied.reshape(orbitals.shape), density)


def solution(mesh):
    placed = (
        P("band", "gy", "gz", None),
        P(("gy", "gz"), None, None),
        P("gy", "gz", None),
        P(None, "gy", "gz", None),
        P(),
        P(),
        P(),
        P(),
        P("band"),
    )
    return jax.shard_map(
        shards,
        mesh=mesh,
        in_specs=placed,
        out_specs=(P("band", "gy", "gz", None), P(("gy", "gz"), None, None)),
        check_vma=False,
    )
```

```python
import functools
import math

import jax
import jax.numpy as jnp
import ml_dtypes
import numpy as np
from jax import lax
from jax.experimental import pallas as pl
from jax.experimental.pallas import tpu as pltpu
from jax.sharding import PartitionSpec as P

kinetic_scale = 1.0 / 1024.0
MESH = pl.DeviceIdType.MESH
F32 = jnp.float32
BF16 = jnp.bfloat16


def dot(a, b, dims):
    return lax.dot_general(a, b, (dims, ((), ())), preferred_element_type=F32)


def parts_of(length, sign_value):
    index = np.arange(length)
    angle = 2.0 * np.pi / length * (index[:, None] * index[None, :] % length)
    cosine = np.cos(angle) / math.sqrt(length)
    sine = sign_value * np.sin(angle) / math.sqrt(length)
    return cosine, sine


def tables(length, rows_z, parts_z):
    group = length // rows_z
    same = np.eye(group)
    out = []
    for sign in (1.0, -1.0):
        c, s = parts_of(length, sign)
        square = np.block([[c, -s], [s, c]])
        out.append(square)
    inv_sq, fwd_sq = out
    order = np.arange(2 * length).reshape(2, length // 8, 8).transpose(1, 0, 2).reshape(-1)
    inv_x = inv_sq[order]
    fwd_x = fwd_sq.T[order]
    c, s = parts_of(length, 1.0)
    z_in = [
        np.einsum("wqz,jk->qjzkw", t.reshape(length, parts_z, rows_z), same).reshape(
            parts_z * group * rows_z, group * length
        )
        for t in (c, s)
    ]
    c, s = parts_of(length, -1.0)
    z_out = [
        np.einsum("qzw,jk->jwqkz", t.reshape(parts_z, rows_z, length), same).reshape(
            group * length, parts_z * group * rows_z
        )
        for t in (c, s)
    ]
    made = (inv_x, np.concatenate(z_in, 1), inv_sq, fwd_sq, np.concatenate(z_out, 1), fwd_x)
    return [np.asarray(t, dtype=np.float32).astype(ml_dtypes.bfloat16) for t in made]


def folds(length, rows):
    group = length // rows
    count = rows // group
    first = np.arange(rows) + length // 4
    inside = first[:, None] ** 2 + first[None, :] ** 2 < (length // 2) ** 2
    width = inside.reshape(count, group, rows).any(axis=1).sum(axis=1)
    kept = [g for g in range(count) if width[g]]
    plan = []
    while kept:
        g = kept.pop(0)
        other = None
        for h in reversed(kept):
            if width[g] + width[h] <= rows:
                other = h
                kept.remove(h)
                break
        plan.append((g, other, int(width[g])))
    dropped = [g for g in range(count) if not width[g]]
    return plan, dropped


def kernel(
    sizes,
    pos_ref,
    atom_ref,
    kind_ref,
    coup_ref,
    occ_ref,
    orb_hbm,
    mask_hbm,
    ix_hbm,
    chan_hbm,
    tz_hbm,
    t2_hbm,
    pot_hbm,
    f2_hbm,
    tb_hbm,
    fx_hbm,
    out_hbm,
    dens_hbm,
    orb_ref,
    mask_ref,
    ix_ref,
    chan_ref,
    tz_ref,
    t2_ref,
    pot_ref,
    f2_ref,
    tb_ref,
    fx_ref,
    out_ref,
    dens_out_ref,
    in_sem,
    out_sem,
    masked,
    tx,
    rx,
    tx2,
    rx2,
    txc,
    rxc,
    txc2,
    rxc2,
    zs,
    dens,
    dens_rx,
    extra,
    phase,
    fold,
    over_tx,
    over_rx,
    send_sem,
    recv_sem,
    over_send,
    over_recv,
    dens_send,
    dens_recv,
):
    N, C, A, length, rows_y, rows_z, py, pz, bands = sizes
    L = 2 * C * N * A
    half = L // 2
    group = length // rows_z
    G = rows_y // group
    S = py * pz
    cols = rows_y * rows_z
    gy = lax.axis_index("gy")
    gz = lax.axis_index("gz")
    band = lax.axis_index("band")
    me = gy * pz + gz

    half_rows = cols
    moves = [
        pltpu.make_async_copy(
            orb_hbm.at[pl.ds(n * half_rows, half_rows)],
            orb_ref.at[pl.ds(n * half_rows, half_rows)],
            in_sem.at[n],
        )
        for n in range(N)
    ]
    held = (
        (ix_hbm, ix_ref),
        (mask_hbm, mask_ref),
        (chan_hbm, chan_ref),
        (tz_hbm, tz_ref),
        (t2_hbm, t2_ref),
        (pot_hbm, pot_ref),
        (f2_hbm, f2_ref),
        (tb_hbm, tb_ref),
        (fx_hbm, fx_ref),
    )
    loads = [pltpu.make_async_copy(a, b, in_sem.at[N + i]) for i, (a, b) in enumerate(held)]
    for move in loads[:2] + moves + loads[2:]:
        move.start()

    def peer(d):
        to = lax.rem(me + d, S)
        return to, {"gy": to // pz, "gz": lax.rem(to, pz)}

    def place_of(to_y, to_z):
        return to_y * pz + to_z, {"gy": to_y, "gz": to_z}

    if pz == 4:
        far = [lax.rem(gz + 2, pz), 3 - gz, gz + 1 - 2 * lax.rem(gz, 2)]
    else:
        far = [lax.rem(gz + k, pz) for k in range(1, pz)]

    barrier = pltpu.get_barrier_semaphore()

    def greet(d, c):
        pl.semaphore_signal(barrier, inc=1, device_id=peer(d)[1], device_id_type=MESH)
        return c

    def greet_band(d, c):
        pl.semaphore_signal(
            barrier, inc=1, device_id={"band": lax.rem(band + d, bands)}, device_id_type=MESH
        )
        return c

    lax.fori_loop(1, S, greet, 0)
    lax.fori_loop(1, bands, greet_band, 0)

    plan, dropped = folds(length, rows_y)
    corner = [k for k in range(pz) if 0 < k < pz - 1]

    def middle(k, parts):
        return (k > 0) & (k < parts - 1)

    def is_corner(y, z):
        return middle(y, py) & middle(z, pz)

    def place_in(t, y):
        return jnp.where(y >= py // 2, G - 1 - t, t)

    def shifted(block, amount, flip):
        return pltpu.roll(block, (128 - amount) % 128 if flip else amount % 128, 1)

    def depth_in(shape, flip):
        z = lax.rem(lax.broadcasted_iota(jnp.int32, shape, 1), rows_z)
        return rows_z - 1 - z if flip else z

    wide_bufs = ((tx, rx), (tx2, rx2))
    slim_bufs = ((txc, rxc), (txc2, rxc2))

    def block_copy(slim, step, n, to, place, slot):
        src, dst = (slim_bufs if slim else wide_bufs)[step]
        return pltpu.make_async_remote_copy(
            src_ref=src.at[to, n],
            dst_ref=dst.at[slot, n],
            send_sem=send_sem.at[step, n, to],
            recv_sem=recv_sem.at[step, n, slot],
            device_id=place,
            device_id_type=MESH,
        )

    def by_kind(slim, act):
        pl.when(slim)(lambda: act(True))
        pl.when(jnp.logical_not(slim))(lambda: act(False))

    def send_row(step, n, d):
        to_y = lax.rem(gy + d, py)
        for to_z in far + [gz]:
            to, place = place_of(to_y, to_z)
            slim = is_corner(gy, gz) if step == 0 else is_corner(to_y, to_z)

            def start():
                by_kind(slim, lambda k: block_copy(k, step, n, to, place, me).start())

            if to_z is gz:
                pl.when(d > 0)(start)
            else:
                start()

    def wait_row(step, n, d):
        from_y = lax.rem(gy + py - d, py)
        for from_z in far + [gz]:
            frm, place = place_of(from_y, from_z)
            slim = is_corner(from_y, from_z) if step == 0 else is_corner(gy, gz)

            def wait():
                by_kind(slim, lambda k: block_copy(k, step, n, frm, place, frm).wait_recv())

            if from_z is gz:
                pl.when(d > 0)(wait)
            else:
                wait()

    def wait_sent(step, n):
        def one(d, c):
            to, place = peer(d)
            to_y, to_z = place["gy"], place["gz"]
            slim = is_corner(gy, gz) if step == 0 else is_corner(to_y, to_z)
            by_kind(slim, lambda k: block_copy(k, step, n, to, place, me).wait_send())
            return c

        lax.fori_loop(1, S, one, 0)

    def fold_mine(n):
        for t, (g, other, width) in enumerate(plan):
            block = tx[:, n, place_in(g, gy)].astype(F32).reshape(S * 16, 128)
            if other is not None:
                more = tx[:, n, place_in(other, gy)].astype(F32).reshape(S * 16, 128)
                block = block + jnp.where(
                    gz >= pz // 2, shifted(more, width, True), shifted(more, width, False)
                )
            txc[:, n, t] = block.astype(BF16).reshape(S, 16, 128)

    def unfold_from(n, y, k):
        s = y * pz + k
        flip = k >= pz // 2
        depth = depth_in((16, 128), flip)
        for t, (g, other, width) in enumerate(plan):
            block = rxc[s, n, t].astype(F32)
            if other is None:
                rx[s, n, place_in(g, y)] = block.astype(BF16)
            else:
                rx[s, n, place_in(g, y)] = jnp.where(depth < width, block, 0.0).astype(BF16)
                more = shifted(block, width, not flip)
                more = jnp.where(depth < rows_z - width, more, 0.0)
                rx[s, n, place_in(other, y)] = more.astype(BF16)
        for g in dropped:
            rx[s, n, place_in(g, y)] = jnp.zeros((16, 128), BF16)

    def fold_for(n, y, k):
        s = y * pz + k
        flip = k >= pz // 2
        depth = depth_in((16, 128), flip)
        for t, (g, other, width) in enumerate(plan):
            block = tx2[s, n, place_in(g, y)].astype(F32)
            if other is not None:
                more = shifted(tx2[s, n, place_in(other, y)].astype(F32), width, flip)
                block = jnp.where(depth < width, block, more)
            txc2[s, n, t] = block.astype(BF16)

    def unfold_mine(n):
        for t, (g, other, width) in enumerate(plan):
            block = rxc2[:, n, t]
            rx2[:, n, place_in(g, gy)] = block
            if other is not None:
                block = block.astype(F32).reshape(S * 16, 128)
                more = jnp.where(
                    gz >= pz // 2, shifted(block, width, False), shifted(block, width, True)
                )
                rx2[:, n, place_in(other, gy)] = more.astype(BF16).reshape(S, 16, 128)
        for g in dropped:
            rx2[:, n, place_in(g, gy)] = jnp.zeros((S, 16, 128), BF16)

    def x_group(n, g, c):
        rows = pl.ds(pl.multiple_of((n * G + g) * 128, 128), 128)
        keep = mask_ref[pl.ds(pl.multiple_of(g * 128, 128), 128), :] != 0
        keep = jnp.concatenate([keep.astype(F32)] * 2, axis=1) != 0
        block = jnp.where(keep, orb_ref[rows, :].astype(F32), 0.0).astype(BF16)
        masked[rows, :] = block
        made = dot(ix_ref[...], block, ((1,), (1,))).astype(BF16)
        tx[:, n, g] = made.reshape(S, 16, 128)
        return c

    loads[0].wait()
    loads[1].wait()
    for n in range(N):
        moves[n].wait()
        lax.fori_loop(0, G, functools.partial(x_group, n), 0)
        if n == 0:
            pl.semaphore_wait(barrier, S - 1 + bands - 1)
        pl.when(is_corner(gy, gz))(functools.partial(fold_mine, n))

        def send_all(d, c):
            send_row(0, n, d)
            return c

        lax.fori_loop(0, py, send_all, 0)
        rx[me, n] = tx[me, n]

    def centred(index):
        return jnp.where(index >= length // 2, index - length, index).astype(F32)

    def turn(amount):
        angle = (2.0 * math.pi) * (amount - jnp.round(amount))
        return jnp.cos(angle), jnp.sin(angle)

    fy = centred(lax.broadcasted_iota(jnp.int32, (rows_y, L), 0) + gy * rows_y)
    fz = centred(lax.broadcasted_iota(jnp.int32, (rows_z, L), 0) + gz * rows_z)
    fx = centred(lax.broadcasted_iota(jnp.int32, (L, length), 1))
    lane = lax.broadcasted_iota(jnp.int32, (1, L), 1)
    lane_atom = lax.rem(lane, A)
    lane_chan = lax.rem(lane, half) // (N * A)
    row_atom = lax.rem(lax.broadcasted_iota(jnp.int32, (L, length), 0), A)
    at_x = jnp.zeros((L, length), F32)
    at_y = jnp.zeros((1, L), F32)
    at_z = jnp.zeros((1, L), F32)
    for a in range(A):
        at_x = jnp.where(row_atom == a, pos_ref[0, a], at_x)
        at_y = jnp.where(lane_atom == a, pos_ref[1, a], at_y)
        at_z = jnp.where(lane_atom == a, pos_ref[2, a], at_z)
    cy, sy = turn(fy * at_y)
    cz, sz = turn(fz * at_z)
    cx, sx = turn(fx * at_x)
    for y in range(rows_y):
        at = pl.ds(y * rows_z, rows_z)
        phase[0, at, :] = cy[y : y + 1] * cz - sy[y : y + 1] * sz
        phase[1, at, :] = sy[y : y + 1] * cz + cy[y : y + 1] * sz
    row = lax.broadcasted_iota(jnp.int32, (L, 2 * length), 0)
    pair = lax.rem(row, half) // A
    real_row = row < half
    cs = jnp.concatenate([cx, -sx], axis=1)
    sc = jnp.concatenate([sx, cx], axis=1)
    wave = jnp.where(real_row, cs, sc)
    for i in range(C * N):
        fold[i] = jnp.where(pair == i, wave, 0.0).astype(BF16)
    sign = jnp.where(lane < half, -1.0, 1.0)

    loads[2].wait()

    def over_group(g, total):
        at = pl.ds(pl.multiple_of(g * 128, 128), 128)
        found = jnp.zeros((128, L), F32)
        for c in range(C):
            profile = chan_ref[c, at, :]
            profile = jnp.concatenate([profile, profile], axis=1)
            for n in range(N):
                rows = pl.ds(pl.multiple_of(n * cols + g * 128, 128), 128)
                found = found + dot(profile * masked[rows, :], fold[c * N + n], ((1,), (1,)))
        swapped = pltpu.roll(found, half, 1)
        value = phase[0, at, :] * found + sign * (phase[1, at, :] * swapped)
        return total + jnp.sum(value, axis=0, keepdims=True)

    total = lax.fori_loop(0, G, over_group, jnp.zeros((1, L), F32))
    over_tx[...] = jnp.broadcast_to(total, (8, L))

    def over_copy(to, place, slot):
        return pltpu.make_async_remote_copy(
            src_ref=over_tx,
            dst_ref=over_rx.at[slot],
            send_sem=over_send.at[to],
            recv_sem=over_recv.at[slot],
            device_id=place,
            device_id_type=MESH,
        )

    def over_start(d, c):
        to, place = peer(d)
        over_copy(to, place, me).start()
        return c

    lax.fori_loop(1, S, over_start, 0)
    over_rx[me] = over_tx[...]

    for move in loads[3:]:
        move.wait()
    for n in range(N):

        def z_in(d, c):
            wait_row(0, n, d)
            q = lax.rem(gy + py - d, py)
            for k in corner:
                pl.when(middle(q, py) & (q * pz + k != me))(
                    functools.partial(unfold_from, n, q, k)
                )
            lhs = jnp.concatenate(
                [rx[q * pz + k, n].reshape(G * 16, 128) for k in range(pz)], axis=1
            )
            made = dot(lhs, tz_ref[...], ((1,), (0,)))
            u = made[:, : group * length].reshape(G, 2, 8, group * length)
            v = made[:, group * length :].reshape(G, 2, 8, group * length)
            re = u[:, 0] - v[:, 1]
            im = v[:, 0] + u[:, 1]
            for g in range(G):
                for j in range(group):
                    at = pl.multiple_of((q * rows_y + g * group + j) * 16, 16)
                    zs[pl.ds(at, 8), :] = re[g, :, j * length : (j + 1) * length]
                    zs[pl.ds(at + 8, 8), :] = im[g, :, j * length : (j + 1) * length]
            return c

        lax.fori_loop(0, py, z_in, 0)
        for x in range(8):
            low = pl.ds(x, length, stride=16)
            high = pl.ds(x + 8, length, stride=16)
            both = jnp.concatenate([zs[low, :], zs[high, :]], axis=0).astype(BF16)
            field = dot(t2_ref[...], both, ((1,), (0,)))
            re, im = field[:length], field[length:]
            weight = occ_ref[n] * (re * re + im * im)
            if n == 0:
                dens[x] = weight
            else:
                dens[x] = dens[x] + weight
            pot = pot_ref[x]
            scaled = jnp.concatenate([pot * re, pot * im], axis=0).astype(BF16)
            back = dot(f2_ref[...], scaled, ((1,), (0,)))
            zs[low, :] = back[:length]
            zs[high, :] = back[length:]

        def z_out(d, c):
            q = lax.rem(gy + d, py)
            at = pl.ds(pl.multiple_of(q * rows_y * 16, 512), rows_y * 16)
            block = zs[at, :].reshape(G, group, 16, length)
            lhs = jnp.concatenate(
                [block[:, j].reshape(G * 16, length) for j in range(group)], axis=1
            ).astype(BF16)
            made = dot(lhs, tb_ref[...], ((1,), (0,)))
            u = made[:, : pz * 128].reshape(G, 2, 8, pz * 128)
            v = made[:, pz * 128 :].reshape(G, 2, 8, pz * 128)
            re = u[:, 0] - v[:, 1]
            im = v[:, 0] + u[:, 1]
            joined = jnp.concatenate([re, im], axis=1).astype(BF16)
            for k in range(pz):
                tx2[q * pz + k, n] = joined[:, :, k * 128 : (k + 1) * 128]
            for k in corner:
                pl.when(middle(q, py))(functools.partial(fold_for, n, q, k))
            send_row(1, n, d)
            return c

        lax.fori_loop(0, py, z_out, 0)

        @pl.when(is_corner(gy, gz))
        def _():
            rxc2[me, n] = txc2[me, n]

        @pl.when(jnp.logical_not(is_corner(gy, gz)))
        def _():
            rx2[me, n] = tx2[me, n]

    dens_rx[band] = dens[...].astype(BF16)

    def dens_copy(d, slot):
        to = lax.rem(band + d, bands)
        return pltpu.make_async_remote_copy(
            src_ref=dens_rx.at[band],
            dst_ref=dens_rx.at[slot],
            send_sem=dens_send.at[to],
            recv_sem=dens_recv.at[slot],
            device_id={"band": to},
            device_id_type=MESH,
        )

    def dens_start(d, c):
        dens_copy(d, band).start()
        return c

    lax.fori_loop(1, bands, dens_start, 0)

    def over_wait(d, c):
        frm, place = peer(d)
        over_copy(frm, place, frm).wait_recv()
        return c

    lax.fori_loop(1, S, over_wait, 0)
    meet = over_rx[0]
    for s in range(1, S):
        meet = meet + over_rx[s]
    meet = meet[0:1]
    coef = jnp.zeros((1, L), F32)
    for p in range(coup_ref.shape[0]):
        hit = (lane_chan == kind_ref[p]) & (lane_atom == atom_ref[p])
        coef = coef + jnp.where(hit, (coup_ref[p] * meet).astype(BF16).astype(F32), 0.0)
    coef_swapped = pltpu.roll(jnp.broadcast_to(coef, (8, L)), half, 1)[0:1]

    def apply_group(g, c):
        at = pl.ds(pl.multiple_of(g * 128, 128), 128)
        lhs = phase[0, at, :] * coef - phase[1, at, :] * (sign * coef_swapped)
        lhs = lhs.astype(BF16)
        index = lax.broadcasted_iota(jnp.int32, (128, length), 0) + g * 128
        ky = centred(gy * rows_y + index // rows_z)
        kz = centred(gz * rows_z + lax.rem(index, rows_z))
        kx = centred(lax.broadcasted_iota(jnp.int32, (128, length), 1))
        energy = (kinetic_scale * 0.5) * (ky * ky + kz * kz + kx * kx)
        energy = jnp.concatenate([energy, energy], axis=1)
        sums = [None] * N
        for n in range(N):
            rows = pl.ds(pl.multiple_of(n * cols + g * 128, 128), 128)
            sums[n] = energy * masked[rows, :].astype(F32)
        for k in range(C):
            profile = chan_ref[k, at, :].astype(F32)
            profile = jnp.concatenate([profile, profile], axis=1)
            for n in range(N):
                sums[n] = sums[n] + profile * dot(lhs, fold[k * N + n], ((1,), (0,)))
        for n in range(N):
            rows = pl.ds(pl.multiple_of(n * cols + g * 128, 128), 128)
            extra[rows, :] = sums[n]
        return c

    lax.fori_loop(0, G, apply_group, 0)

    def dens_wait(d, c):
        dens_copy(d, lax.rem(band + d, bands)).wait_recv()
        return c

    lax.fori_loop(1, bands, dens_wait, 0)
    whole = dens_rx[0].astype(F32)
    for b in range(1, bands):
        whole = whole + dens_rx[b].astype(F32)
    dens_out_ref[...] = whole
    dens_move = pltpu.make_async_copy(dens_out_ref, dens_hbm, out_sem.at[N])
    dens_move.start()

    leaves = []
    for n in range(N):
        def arrive(d, c):
            wait_row(1, n, d)
            return c

        lax.fori_loop(0, py, arrive, 0)
        pl.when(is_corner(gy, gz))(functools.partial(unfold_mine, n))

        def finish(g, c):
            rows = pl.ds(pl.multiple_of((n * G + g) * 128, 128), 128)
            keep = mask_ref[pl.ds(pl.multiple_of(g * 128, 128), 128), :] != 0
            keep = jnp.concatenate([keep.astype(F32)] * 2, axis=1) != 0
            block = rx2[:, n, g].reshape(S * 16, 128)
            local = dot(block, fx_ref[...], ((0,), (0,)))
            out_ref[rows, :] = jnp.where(keep, local + extra[rows, :], 0.0).astype(BF16)
            return c

        lax.fori_loop(0, G, finish, 0)
        span = pl.ds(n * half_rows, half_rows)
        leave = pltpu.make_async_copy(out_ref.at[span], out_hbm.at[span], out_sem.at[n])
        leave.start()
        leaves.append(leave)

    for n in range(N):
        wait_sent(0, n)
        wait_sent(1, n)

    def over_done(d, c):
        to, place = peer(d)
        over_copy(to, place, me).wait_send()
        return c

    lax.fori_loop(1, S, over_done, 0)

    def dens_done(d, c):
        dens_copy(d, band).wait_send()
        return c

    lax.fori_loop(1, bands, dens_done, 0)
    dens_move.wait()
    for leave in leaves:
        leave.wait()


def hand_on(pieces, *refs):
    ins, outs, held = refs[:2], refs[2:4], refs[4:6]
    sem_in, sem_out = refs[6:]
    steps = []
    for i in range(2):
        rows = ins[i].shape[0] // pieces
        for k in range(pieces):
            span = pl.ds(k * rows, rows)
            here = held[i].at[span]
            steps.append(
                (
                    pltpu.make_async_copy(ins[i].at[span], here, sem_in.at[i, k]),
                    pltpu.make_async_copy(here, outs[i].at[span], sem_out.at[i, k]),
                )
            )
    for read, _ in steps:
        read.start()
    for read, write in steps:
        read.wait()
        write.start()
    for _, write in steps:
        write.wait()


def shards(
    orbitals,
    potential,
    cutoff_mask,
    channels,
    positions,
    proj_atom,
    proj_chan,
    coupling,
    occupations,
):
    N, rows_y, rows_z, wide = orbitals.shape
    length = wide // 2
    C = channels.shape[0]
    A = positions.shape[0]
    py, pz, bands = lax.axis_size("gy"), lax.axis_size("gz"), lax.axis_size("band")
    S = py * pz
    L = 2 * C * N * A
    G = rows_y * rows_z // 128
    cols = rows_y * rows_z
    ix, tz, t2, f2, tb, fx = [jnp.asarray(t) for t in tables(length, rows_z, pz)]
    hbm = pl.BlockSpec(memory_space=pl.ANY)
    smem = pl.BlockSpec(memory_space=pltpu.SMEM)
    sizes = (N, C, A, length, rows_y, rows_z, py, pz, bands)
    planes = (S, N, G, 16, 128)
    slim = (S, N, len(folds(length, rows_y)[0]), 16, 128)
    applied, density = pl.pallas_call(
        functools.partial(kernel, sizes),
        out_shape=(
            jax.ShapeDtypeStruct((N * cols, wide), BF16),
            jax.ShapeDtypeStruct(potential.shape, F32),
        ),
        in_specs=[smem] * 5 + [hbm] * 10,
        out_specs=(hbm, hbm),
        scratch_shapes=[
            pltpu.VMEM((N * cols, wide), BF16),
            pltpu.VMEM((cols, length), jnp.int32),
            pltpu.VMEM(ix.shape, BF16),
            pltpu.VMEM((C, cols, length), BF16),
            pltpu.VMEM(tz.shape, BF16),
            pltpu.VMEM(t2.shape, BF16),
            pltpu.VMEM(potential.shape, F32),
            pltpu.VMEM(f2.shape, BF16),
            pltpu.VMEM(tb.shape, BF16),
            pltpu.VMEM(fx.shape, BF16),
            pltpu.VMEM((N * cols, wide), BF16),
            pltpu.VMEM(potential.shape, F32),
            pltpu.SemaphoreType.DMA((N + 9,)),
            pltpu.SemaphoreType.DMA((N + 1,)),
            pltpu.VMEM((N * cols, wide), BF16),
            pltpu.VMEM(planes, BF16),
            pltpu.VMEM(planes, BF16),
            pltpu.VMEM(planes, BF16),
            pltpu.VMEM(planes, BF16),
            pltpu.VMEM(slim, BF16),
            pltpu.VMEM(slim, BF16),
            pltpu.VMEM(slim, BF16),
            pltpu.VMEM(slim, BF16),
            pltpu.VMEM((length * 16, length), F32),
            pltpu.VMEM(potential.shape, F32),
            pltpu.VMEM((bands,) + potential.shape, BF16),
            pltpu.VMEM((N * cols, wide), F32),
            pltpu.VMEM((2, cols, L), F32),
            pltpu.VMEM((C * N, L, wide), BF16),
            pltpu.VMEM((8, L), F32),
            pltpu.VMEM((S, 8, L), F32),
            pltpu.SemaphoreType.DMA((2, N, S)),
            pltpu.SemaphoreType.DMA((2, N, S)),
            pltpu.SemaphoreType.DMA((S,)),
            pltpu.SemaphoreType.DMA((S,)),
            pltpu.SemaphoreType.DMA((bands,)),
            pltpu.SemaphoreType.DMA((bands,)),
        ],
        compiler_params=pltpu.CompilerParams(
            collective_id=0, has_side_effects=True, vmem_limit_bytes=56 * 1024 * 1024
        ),
    )(
        positions.T,
        proj_atom,
        proj_chan,
        coupling,
        occupations,
        orbitals.reshape(N * cols, wide),
        cutoff_mask.reshape(cols, length),
        ix,
        channels.reshape(C, cols, length),
        tz,
        t2,
        potential,
        f2,
        tb,
        fx,
    )
    pieces = 4
    applied, density = pl.pallas_call(
        functools.partial(hand_on, pieces),
        out_shape=(
            jax.ShapeDtypeStruct((N * cols, wide), BF16),
            jax.ShapeDtypeStruct(potential.shape, F32),
        ),
        in_specs=[hbm] * 2,
        out_specs=(hbm, hbm),
        scratch_shapes=[
            pltpu.VMEM((N * cols, wide), BF16),
            pltpu.VMEM(potential.shape, F32),
            pltpu.SemaphoreType.DMA((2, pieces)),
            pltpu.SemaphoreType.DMA((2, pieces)),
        ],
    )(applied, density)
    return (applied.reshape(orbitals.shape), density)


def solution(mesh):
    placed = (
        P("band", "gy", "gz", None),
        P(("gy", "gz"), None, None),
        P("gy", "gz", None),
        P(None, "gy", "gz", None),
        P(),
        P(),
        P(),
        P(),
        P("band"),
    )
    return jax.shard_map(
        shards,
        mesh=mesh,
        in_specs=placed,
        out_specs=(P("band", "gy", "gz", None), P(("gy", "gz"), None, None)),
        check_vma=False,
    )
```

```python
import functools
import math

import jax
import jax.numpy as jnp
import ml_dtypes
import numpy as np
from jax import lax
from jax.experimental import pallas as pl
from jax.experimental.pallas import tpu as pltpu
from jax.sharding import PartitionSpec as P

kinetic_scale = 1.0 / 1024.0
MESH = pl.DeviceIdType.MESH
F32 = jnp.float32
BF16 = jnp.bfloat16


def dot(a, b, dims):
    return lax.dot_general(a, b, (dims, ((), ())), preferred_element_type=F32)


def parts_of(length, sign_value):
    index = np.arange(length)
    angle = 2.0 * np.pi / length * (index[:, None] * index[None, :] % length)
    cosine = np.cos(angle) / math.sqrt(length)
    sine = sign_value * np.sin(angle) / math.sqrt(length)
    return cosine, sine


def tables(length, rows_z, parts_z):
    group = length // rows_z
    same = np.eye(group)
    out = []
    for sign in (1.0, -1.0):
        c, s = parts_of(length, sign)
        square = np.block([[c, -s], [s, c]])
        out.append(square)
    inv_sq, fwd_sq = out
    order = np.arange(2 * length).reshape(2, length // 8, 8).transpose(1, 0, 2).reshape(-1)
    inv_x = inv_sq[order]
    fwd_x = fwd_sq.T[order]
    c, s = parts_of(length, 1.0)
    z_in = [
        np.einsum("wqz,jk->qjzkw", t.reshape(length, parts_z, rows_z), same).reshape(
            parts_z * group * rows_z, group * length
        )
        for t in (c, s)
    ]
    c, s = parts_of(length, -1.0)
    z_out = [
        np.einsum("qzw,jk->jwqkz", t.reshape(parts_z, rows_z, length), same).reshape(
            group * length, parts_z * group * rows_z
        )
        for t in (c, s)
    ]
    made = (inv_x, np.concatenate(z_in, 1), inv_sq, fwd_sq, np.concatenate(z_out, 1), fwd_x)
    return [np.asarray(t, dtype=np.float32).astype(ml_dtypes.bfloat16) for t in made]


def folds(length, rows):
    group = length // rows
    count = rows // group
    first = np.arange(rows) + length // 4
    inside = first[:, None] ** 2 + first[None, :] ** 2 < (length // 2) ** 2
    width = inside.reshape(count, group, rows).any(axis=1).sum(axis=1)
    kept = [g for g in range(count) if width[g]]
    plan = []
    while kept:
        g = kept.pop(0)
        other = None
        for h in reversed(kept):
            if width[g] + width[h] <= rows:
                other = h
                kept.remove(h)
                break
        plan.append((g, other, int(width[g])))
    dropped = [g for g in range(count) if not width[g]]
    return plan, dropped


def kernel(
    sizes,
    pos_ref,
    atom_ref,
    kind_ref,
    coup_ref,
    occ_ref,
    orb_hbm,
    mask_hbm,
    ix_hbm,
    chan_hbm,
    tz_hbm,
    t2_hbm,
    pot_hbm,
    f2_hbm,
    tb_hbm,
    fx_hbm,
    out_hbm,
    dens_hbm,
    orb_ref,
    mask_ref,
    ix_ref,
    chan_ref,
    tz_ref,
    t2_ref,
    pot_ref,
    f2_ref,
    tb_ref,
    fx_ref,
    out_ref,
    dens_out_ref,
    in_sem,
    out_sem,
    masked,
    tx,
    rx,
    tx2,
    rx2,
    txc,
    rxc,
    txc2,
    rxc2,
    zs,
    dens,
    dens_rx,
    extra,
    phase,
    fold,
    foldt,
    weighed,
    over_tx,
    over_rx,
    send_sem,
    recv_sem,
    over_send,
    over_recv,
    dens_send,
    dens_recv,
):
    N, C, A, length, rows_y, rows_z, py, pz, bands = sizes
    L = 2 * C * N * A
    half = L // 2
    group = length // rows_z
    G = rows_y // group
    S = py * pz
    cols = rows_y * rows_z
    gy = lax.axis_index("gy")
    gz = lax.axis_index("gz")
    band = lax.axis_index("band")
    me = gy * pz + gz

    half_rows = cols
    moves = [
        pltpu.make_async_copy(
            orb_hbm.at[pl.ds(n * half_rows, half_rows)],
            orb_ref.at[pl.ds(n * half_rows, half_rows)],
            in_sem.at[n],
        )
        for n in range(N)
    ]
    held = (
        (ix_hbm, ix_ref),
        (mask_hbm, mask_ref),
        (chan_hbm, chan_ref),
        (tz_hbm, tz_ref),
        (t2_hbm, t2_ref),
        (pot_hbm, pot_ref),
        (f2_hbm, f2_ref),
        (tb_hbm, tb_ref),
        (fx_hbm, fx_ref),
    )
    loads = [pltpu.make_async_copy(a, b, in_sem.at[N + i]) for i, (a, b) in enumerate(held)]
    for move in loads[:2] + moves + loads[2:]:
        move.start()

    def peer(d):
        to = lax.rem(me + d, S)
        return to, {"gy": to // pz, "gz": lax.rem(to, pz)}

    def place_of(to_y, to_z):
        return to_y * pz + to_z, {"gy": to_y, "gz": to_z}

    if pz == 4:
        far = [lax.rem(gz + 2, pz), 3 - gz, gz + 1 - 2 * lax.rem(gz, 2)]
    else:
        far = [lax.rem(gz + k, pz) for k in range(1, pz)]

    barrier = pltpu.get_barrier_semaphore()

    def greet(d, c):
        pl.semaphore_signal(barrier, inc=1, device_id=peer(d)[1], device_id_type=MESH)
        return c

    def greet_band(d, c):
        pl.semaphore_signal(
            barrier, inc=1, device_id={"band": lax.rem(band + d, bands)}, device_id_type=MESH
        )
        return c

    lax.fori_loop(1, S, greet, 0)
    lax.fori_loop(1, bands, greet_band, 0)

    plan, dropped = folds(length, rows_y)
    corner = [k for k in range(pz) if 0 < k < pz - 1]

    def middle(k, parts):
        return (k > 0) & (k < parts - 1)

    def is_corner(y, z):
        return middle(y, py) & middle(z, pz)

    def place_in(t, y):
        return jnp.where(y >= py // 2, G - 1 - t, t)

    def shifted(block, amount, flip):
        return pltpu.roll(block, (128 - amount) % 128 if flip else amount % 128, 1)

    def depth_in(shape, flip):
        z = lax.rem(lax.broadcasted_iota(jnp.int32, shape, 1), rows_z)
        return rows_z - 1 - z if flip else z

    wide_bufs = ((tx, rx), (tx2, rx2))
    slim_bufs = ((txc, rxc), (txc2, rxc2))

    def block_copy(slim, step, n, to, place, slot):
        src, dst = (slim_bufs if slim else wide_bufs)[step]
        return pltpu.make_async_remote_copy(
            src_ref=src.at[to, n],
            dst_ref=dst.at[slot, n],
            send_sem=send_sem.at[step, n, to],
            recv_sem=recv_sem.at[step, n, slot],
            device_id=place,
            device_id_type=MESH,
        )

    def by_kind(slim, act):
        pl.when(slim)(lambda: act(True))
        pl.when(jnp.logical_not(slim))(lambda: act(False))

    def send_row(step, n, d):
        to_y = lax.rem(gy + d, py)
        for to_z in far + [gz]:
            to, place = place_of(to_y, to_z)
            slim = is_corner(gy, gz) if step == 0 else is_corner(to_y, to_z)

            def start():
                by_kind(slim, lambda k: block_copy(k, step, n, to, place, me).start())

            if to_z is gz:
                pl.when(d > 0)(start)
            else:
                start()

    def wait_row(step, n, d):
        from_y = lax.rem(gy + py - d, py)
        for from_z in far + [gz]:
            frm, place = place_of(from_y, from_z)
            slim = is_corner(from_y, from_z) if step == 0 else is_corner(gy, gz)

            def wait():
                by_kind(slim, lambda k: block_copy(k, step, n, frm, place, frm).wait_recv())

            if from_z is gz:
                pl.when(d > 0)(wait)
            else:
                wait()

    def wait_sent(step, n):
        def one(d, c):
            to, place = peer(d)
            to_y, to_z = place["gy"], place["gz"]
            slim = is_corner(gy, gz) if step == 0 else is_corner(to_y, to_z)
            by_kind(slim, lambda k: block_copy(k, step, n, to, place, me).wait_send())
            return c

        lax.fori_loop(1, S, one, 0)

    def fold_mine(n):
        for t, (g, other, width) in enumerate(plan):
            block = tx[:, n, place_in(g, gy)].astype(F32).reshape(S * 16, 128)
            if other is not None:
                more = tx[:, n, place_in(other, gy)].astype(F32).reshape(S * 16, 128)
                block = block + jnp.where(
                    gz >= pz // 2, shifted(more, width, True), shifted(more, width, False)
                )
            txc[:, n, t] = block.astype(BF16).reshape(S, 16, 128)

    def unfold_from(n, y, k):
        s = y * pz + k
        flip = k >= pz // 2
        depth = depth_in((16, 128), flip)
        for t, (g, other, width) in enumerate(plan):
            block = rxc[s, n, t].astype(F32)
            if other is None:
                rx[s, n, place_in(g, y)] = block.astype(BF16)
            else:
                rx[s, n, place_in(g, y)] = jnp.where(depth < width, block, 0.0).astype(BF16)
                more = shifted(block, width, not flip)
                more = jnp.where(depth < rows_z - width, more, 0.0)
                rx[s, n, place_in(other, y)] = more.astype(BF16)
        for g in dropped:
            rx[s, n, place_in(g, y)] = jnp.zeros((16, 128), BF16)

    def fold_for(n, y, k):
        s = y * pz + k
        flip = k >= pz // 2
        depth = depth_in((16, 128), flip)
        for t, (g, other, width) in enumerate(plan):
            block = tx2[s, n, place_in(g, y)].astype(F32)
            if other is not None:
                more = shifted(tx2[s, n, place_in(other, y)].astype(F32), width, flip)
                block = jnp.where(depth < width, block, more)
            txc2[s, n, t] = block.astype(BF16)

    def unfold_mine(n):
        for t, (g, other, width) in enumerate(plan):
            block = rxc2[:, n, t]
            rx2[:, n, place_in(g, gy)] = block
            if other is not None:
                block = block.astype(F32).reshape(S * 16, 128)
                more = jnp.where(
                    gz >= pz // 2, shifted(block, width, False), shifted(block, width, True)
                )
                rx2[:, n, place_in(other, gy)] = more.astype(BF16).reshape(S, 16, 128)
        for g in dropped:
            rx2[:, n, place_in(g, gy)] = jnp.zeros((S, 16, 128), BF16)

    def x_group(n, h, c):
        rows = pl.ds(pl.multiple_of(n * cols + h * 256, 256), 256)
        keep = mask_ref[pl.ds(pl.multiple_of(h * 256, 256), 256), :] != 0
        for part in range(2):
            span = pl.ds(part * length, length)
            block = jnp.where(keep, orb_ref[rows, span].astype(F32), 0.0)
            masked[rows, span] = block.astype(BF16)
        made = dot(ix_ref[...], masked[rows, :], ((1,), (1,))).astype(BF16)
        tx[:, n, 2 * h] = made[:, :128].reshape(S, 16, 128)
        tx[:, n, 2 * h + 1] = made[:, 128:].reshape(S, 16, 128)
        return c

    loads[0].wait()
    loads[1].wait()
    for n in range(N):
        moves[n].wait()
        lax.fori_loop(0, G // 2, functools.partial(x_group, n), 0)
        if n == 0:
            pl.semaphore_wait(barrier, S - 1 + bands - 1)
        pl.when(is_corner(gy, gz))(functools.partial(fold_mine, n))

        def send_all(d, c):
            send_row(0, n, d)
            return c

        lax.fori_loop(0, py, send_all, 0)
        rx[me, n] = tx[me, n]

    def centred(index):
        return jnp.where(index >= length // 2, index - length, index).astype(F32)

    def turn(amount):
        quarter = jnp.round(amount * 4.0)
        rest = (2.0 * math.pi) * (amount - 0.25 * quarter)
        sq = rest * rest
        cosine = 1.0 + sq * (
            -0.5 + sq * (1.0 / 24 + sq * (-1.0 / 720 + sq * (1.0 / 40320 - sq * (1.0 / 3628800))))
        )
        sine = rest * (
            1.0
            + sq * (-1.0 / 6 + sq * (1.0 / 120 + sq * (-1.0 / 5040 + sq * (1.0 / 362880))))
        )
        left = quarter - 4.0 * jnp.floor(quarter * 0.25)
        odd = (left == 1.0) | (left == 3.0)
        first = jnp.where(odd, sine, cosine)
        second = jnp.where(odd, cosine, sine)
        first = jnp.where((left == 1.0) | (left == 2.0), -first, first)
        second = jnp.where(left >= 2.0, -second, second)
        return first, second

    fy = centred(lax.broadcasted_iota(jnp.int32, (rows_y, L), 0) + gy * rows_y)
    fz = centred(lax.broadcasted_iota(jnp.int32, (rows_z, L), 0) + gz * rows_z)
    fx = centred(lax.broadcasted_iota(jnp.int32, (L, length), 1))
    lane = lax.broadcasted_iota(jnp.int32, (1, L), 1)
    lane_atom = lax.rem(lane, A)
    lane_chan = lax.rem(lane, half) // (N * A)
    row_atom = lax.rem(lax.broadcasted_iota(jnp.int32, (L, length), 0), A)
    at_x = jnp.zeros((L, length), F32)
    at_y = jnp.zeros((1, L), F32)
    at_z = jnp.zeros((1, L), F32)
    for a in range(A):
        at_x = jnp.where(row_atom == a, pos_ref[0, a], at_x)
        at_y = jnp.where(lane_atom == a, pos_ref[1, a], at_y)
        at_z = jnp.where(lane_atom == a, pos_ref[2, a], at_z)
    cy, sy = turn(fy * at_y)
    cz, sz = turn(fz * at_z)
    cx, sx = turn(fx * at_x)
    for y in range(rows_y):
        at = pl.ds(y * rows_z, rows_z)
        phase[0, at, :] = cy[y : y + 1] * cz - sy[y : y + 1] * sz
        phase[1, at, :] = sy[y : y + 1] * cz + cy[y : y + 1] * sz
    row = lax.broadcasted_iota(jnp.int32, (L, length), 0)
    pair = lax.rem(row, half) // A
    waves = (jnp.where(row < half, cx, sx), jnp.where(row < half, -sx, cx))
    lane_pair = lax.rem(lax.broadcasted_iota(jnp.int32, (length, L), 1), half) // A
    for part in range(2):
        turned = waves[part].T
        for i in range(C * N):
            at = i * 2 * length + part * length
            fold[:, pl.ds(at, length)] = jnp.where(pair == i, waves[part], 0.0).astype(BF16)
            foldt[pl.ds(at, length), :] = jnp.where(lane_pair == i, turned, 0.0).astype(BF16)
    sign = jnp.where(lane < half, -1.0, 1.0)

    loads[2].wait()

    def over_group(h, total):
        at = pl.ds(pl.multiple_of(h * 256, 256), 256)
        for c in range(C):
            profile = chan_ref[c, at, :]
            for n in range(N):
                rows = pl.ds(pl.multiple_of(n * cols + h * 256, 256), 256)
                for part in range(2):
                    lanes = pl.ds(((c * N + n) * 2 + part) * length, length)
                    weighed[:, lanes] = profile * masked[rows, pl.ds(part * length, length)]
        found = dot(weighed[...], foldt[...], ((1,), (0,)))
        swapped = pltpu.roll(found, half, 1)
        value = phase[0, at, :] * found + sign * (phase[1, at, :] * swapped)
        return total + jnp.sum(value, axis=0, keepdims=True)

    total = lax.fori_loop(0, G // 2, over_group, jnp.zeros((1, L), F32))
    over_tx[...] = jnp.broadcast_to(total, (8, L))

    def over_copy(to, place, slot):
        return pltpu.make_async_remote_copy(
            src_ref=over_tx,
            dst_ref=over_rx.at[slot],
            send_sem=over_send.at[to],
            recv_sem=over_recv.at[slot],
            device_id=place,
            device_id_type=MESH,
        )

    def over_start(d, c):
        to, place = peer(d)
        over_copy(to, place, me).start()
        return c

    lax.fori_loop(1, S, over_start, 0)
    over_rx[me] = over_tx[...]

    for move in loads[3:]:
        move.wait()
    for n in range(N):

        def z_in(d, c):
            wait_row(0, n, d)
            q = lax.rem(gy + py - d, py)
            for k in corner:
                pl.when(middle(q, py) & (q * pz + k != me))(
                    functools.partial(unfold_from, n, q, k)
                )
            lhs = jnp.concatenate(
                [rx[q * pz + k, n].reshape(G * 16, 128) for k in range(pz)], axis=1
            )
            made = dot(lhs, tz_ref[...], ((1,), (0,)))
            u = made[:, : group * length].reshape(G, 2, 8, group * length)
            v = made[:, group * length :].reshape(G, 2, 8, group * length)
            re = u[:, 0] - v[:, 1]
            im = v[:, 0] + u[:, 1]
            for g in range(G):
                for j in range(group):
                    at = pl.multiple_of((q * rows_y + g * group + j) * 16, 16)
                    zs[pl.ds(at, 8), :] = re[g, :, j * length : (j + 1) * length]
                    zs[pl.ds(at + 8, 8), :] = im[g, :, j * length : (j + 1) * length]
            return c

        lax.fori_loop(0, py, z_in, 0)
        for x in range(0, 8, 2):
            spans = [pl.ds(x + i, length, stride=16) for i in (0, 1, 8, 9)]
            got = [zs[span, :] for span in spans]
            both = jnp.concatenate(
                [jnp.concatenate(got[:2], axis=1), jnp.concatenate(got[2:], axis=1)], axis=0
            ).astype(BF16)
            field = dot(t2_ref[...], both, ((1,), (0,)))
            ends = []
            for i in range(2):
                lanes = slice(i * length, (i + 1) * length)
                re, im = field[:length, lanes], field[length:, lanes]
                weight = occ_ref[n] * (re * re + im * im)
                dens[x + i] = weight if n == 0 else dens[x + i] + weight
                pot = pot_ref[x + i]
                ends.append(jnp.concatenate([pot * re, pot * im], axis=0).astype(BF16))
            back = dot(f2_ref[...], jnp.concatenate(ends, axis=1), ((1,), (0,)))
            zs[spans[0], :] = back[:length, :length]
            zs[spans[1], :] = back[:length, length:]
            zs[spans[2], :] = back[length:, :length]
            zs[spans[3], :] = back[length:, length:]

        def z_out(d, c):
            q = lax.rem(gy + d, py)
            at = pl.ds(pl.multiple_of(q * rows_y * 16, 512), rows_y * 16)
            block = zs[at, :].reshape(G, group, 16, length)
            lhs = jnp.concatenate(
                [block[:, j].reshape(G * 16, length) for j in range(group)], axis=1
            ).astype(BF16)
            made = dot(lhs, tb_ref[...], ((1,), (0,)))
            u = made[:, : pz * 128].reshape(G, 2, 8, pz * 128)
            v = made[:, pz * 128 :].reshape(G, 2, 8, pz * 128)
            re = u[:, 0] - v[:, 1]
            im = v[:, 0] + u[:, 1]
            joined = jnp.concatenate([re, im], axis=1).astype(BF16)
            for k in range(pz):
                tx2[q * pz + k, n] = joined[:, :, k * 128 : (k + 1) * 128]
            for k in corner:
                pl.when(middle(q, py))(functools.partial(fold_for, n, q, k))
            send_row(1, n, d)
            return c

        lax.fori_loop(0, py, z_out, 0)

        @pl.when(is_corner(gy, gz))
        def _():
            rxc2[me, n] = txc2[me, n]

        @pl.when(jnp.logical_not(is_corner(gy, gz)))
        def _():
            rx2[me, n] = tx2[me, n]

    dens_rx[band] = dens[...].astype(BF16)

    def dens_copy(d, slot):
        to = lax.rem(band + d, bands)
        return pltpu.make_async_remote_copy(
            src_ref=dens_rx.at[band],
            dst_ref=dens_rx.at[slot],
            send_sem=dens_send.at[to],
            recv_sem=dens_recv.at[slot],
            device_id={"band": to},
            device_id_type=MESH,
        )

    def dens_start(d, c):
        dens_copy(d, band).start()
        return c

    lax.fori_loop(1, bands, dens_start, 0)

    def over_wait(d, c):
        frm, place = peer(d)
        over_copy(frm, place, frm).wait_recv()
        return c

    lax.fori_loop(1, S, over_wait, 0)
    meet = over_rx[0]
    for s in range(1, S):
        meet = meet + over_rx[s]
    meet = meet[0:1]
    coef = jnp.zeros((1, L), F32)
    for p in range(coup_ref.shape[0]):
        hit = (lane_chan == kind_ref[p]) & (lane_atom == atom_ref[p])
        coef = coef + jnp.where(hit, (coup_ref[p] * meet).astype(BF16).astype(F32), 0.0)
    coef_swapped = pltpu.roll(jnp.broadcast_to(coef, (8, L)), half, 1)[0:1]

    def apply_group(h, c):
        at = pl.ds(pl.multiple_of(h * 256, 256), 256)
        lhs = phase[0, at, :] * coef - phase[1, at, :] * (sign * coef_swapped)
        lhs = lhs.astype(BF16)
        index = lax.broadcasted_iota(jnp.int32, (256, length), 0) + h * 256
        ky = centred(gy * rows_y + index // rows_z)
        kz = centred(gz * rows_z + lax.rem(index, rows_z))
        kx = centred(lax.broadcasted_iota(jnp.int32, (256, length), 1))
        energy = (kinetic_scale * 0.5) * (ky * ky + kz * kz + kx * kx)
        for n in range(N):
            rows = pl.ds(pl.multiple_of(n * cols + h * 256, 256), 256)
            parts = [
                energy * masked[rows, pl.ds(part * length, length)].astype(F32)
                for part in range(2)
            ]
            for k in range(C):
                profile = chan_ref[k, at, :].astype(F32)
                made = dot(
                    lhs, fold[:, pl.ds((k * N + n) * 2 * length, 2 * length)], ((1,), (0,))
                )
                parts[0] = parts[0] + profile * made[:, :length]
                parts[1] = parts[1] + profile * made[:, length:]
            for part in range(2):
                extra[rows, pl.ds(part * length, length)] = parts[part]
        return c

    lax.fori_loop(0, G // 2, apply_group, 0)

    def dens_wait(d, c):
        dens_copy(d, lax.rem(band + d, bands)).wait_recv()
        return c

    lax.fori_loop(1, bands, dens_wait, 0)
    whole = dens_rx[0].astype(F32)
    for b in range(1, bands):
        whole = whole + dens_rx[b].astype(F32)
    dens_out_ref[...] = whole
    dens_move = pltpu.make_async_copy(dens_out_ref, dens_hbm, out_sem.at[N])
    dens_move.start()

    leaves = []
    for n in range(N):
        def arrive(d, c):
            wait_row(1, n, d)
            return c

        lax.fori_loop(0, py, arrive, 0)
        pl.when(is_corner(gy, gz))(functools.partial(unfold_mine, n))

        def finish(h, c):
            rows = pl.ds(pl.multiple_of(n * cols + h * 256, 256), 256)
            keep = mask_ref[pl.ds(pl.multiple_of(h * 256, 256), 256), :] != 0
            block = jnp.concatenate(
                [rx2[:, n, 2 * h + i].reshape(S * 16, 128) for i in range(2)], axis=1
            )
            local = dot(block, fx_ref[...], ((0,), (0,)))
            for part in range(2):
                lanes = pl.ds(part * length, length)
                value = local[:, part * length : (part + 1) * length] + extra[rows, lanes]
                out_ref[rows, lanes] = jnp.where(keep, value, 0.0).astype(BF16)
            return c

        lax.fori_loop(0, G // 2, finish, 0)
        span = pl.ds(n * half_rows, half_rows)
        leave = pltpu.make_async_copy(out_ref.at[span], out_hbm.at[span], out_sem.at[n])
        leave.start()
        leaves.append(leave)

    for n in range(N):
        wait_sent(0, n)
        wait_sent(1, n)

    def over_done(d, c):
        to, place = peer(d)
        over_copy(to, place, me).wait_send()
        return c

    lax.fori_loop(1, S, over_done, 0)

    def dens_done(d, c):
        dens_copy(d, band).wait_send()
        return c

    lax.fori_loop(1, bands, dens_done, 0)
    dens_move.wait()
    for leave in leaves:
        leave.wait()


def hand_on(pieces, *refs):
    ins, outs, held = refs[:2], refs[2:4], refs[4:6]
    sem_in, sem_out = refs[6:]
    steps = []
    for i in range(2):
        rows = ins[i].shape[0] // pieces
        for k in range(pieces):
            span = pl.ds(k * rows, rows)
            here = held[i].at[span]
            steps.append(
                (
                    pltpu.make_async_copy(ins[i].at[span], here, sem_in.at[i, k]),
                    pltpu.make_async_copy(here, outs[i].at[span], sem_out.at[i, k]),
                )
            )
    for read, _ in steps:
        read.start()
    for read, write in steps:
        read.wait()
        write.start()
    for _, write in steps:
        write.wait()


def shards(
    orbitals,
    potential,
    cutoff_mask,
    channels,
    positions,
    proj_atom,
    proj_chan,
    coupling,
    occupations,
):
    N, rows_y, rows_z, wide = orbitals.shape
    length = wide // 2
    C = channels.shape[0]
    A = positions.shape[0]
    py, pz, bands = lax.axis_size("gy"), lax.axis_size("gz"), lax.axis_size("band")
    S = py * pz
    L = 2 * C * N * A
    G = rows_y * rows_z // 128
    cols = rows_y * rows_z
    ix, tz, t2, f2, tb, fx = [jnp.asarray(t) for t in tables(length, rows_z, pz)]
    hbm = pl.BlockSpec(memory_space=pl.ANY)
    smem = pl.BlockSpec(memory_space=pltpu.SMEM)
    sizes = (N, C, A, length, rows_y, rows_z, py, pz, bands)
    planes = (S, N, G, 16, 128)
    slim = (S, N, len(folds(length, rows_y)[0]), 16, 128)
    applied, density = pl.pallas_call(
        functools.partial(kernel, sizes),
        out_shape=(
            jax.ShapeDtypeStruct((N * cols, wide), BF16),
            jax.ShapeDtypeStruct(potential.shape, F32),
        ),
        in_specs=[smem] * 5 + [hbm] * 10,
        out_specs=(hbm, hbm),
        scratch_shapes=[
            pltpu.VMEM((N * cols, wide), BF16),
            pltpu.VMEM((cols, length), jnp.int32),
            pltpu.VMEM(ix.shape, BF16),
            pltpu.VMEM((C, cols, length), BF16),
            pltpu.VMEM(tz.shape, BF16),
            pltpu.VMEM(t2.shape, BF16),
            pltpu.VMEM(potential.shape, F32),
            pltpu.VMEM(f2.shape, BF16),
            pltpu.VMEM(tb.shape, BF16),
            pltpu.VMEM(fx.shape, BF16),
            pltpu.VMEM((N * cols, wide), BF16),
            pltpu.VMEM(potential.shape, F32),
            pltpu.SemaphoreType.DMA((N + 9,)),
            pltpu.SemaphoreType.DMA((N + 1,)),
            pltpu.VMEM((N * cols, wide), BF16),
            pltpu.VMEM(planes, BF16),
            pltpu.VMEM(planes, BF16),
            pltpu.VMEM(planes, BF16),
            pltpu.VMEM(planes, BF16),
            pltpu.VMEM(slim, BF16),
            pltpu.VMEM(slim, BF16),
            pltpu.VMEM(slim, BF16),
            pltpu.VMEM(slim, BF16),
            pltpu.VMEM((length * 16, length), F32),
            pltpu.VMEM(potential.shape, F32),
            pltpu.VMEM((bands,) + potential.shape, BF16),
            pltpu.VMEM((N * cols, wide), F32),
            pltpu.VMEM((2, cols, L), F32),
            pltpu.VMEM((L, C * N * wide), BF16),
            pltpu.VMEM((C * N * wide, L), BF16),
            pltpu.VMEM((256, C * N * wide), BF16),
            pltpu.VMEM((8, L), F32),
            pltpu.VMEM((S, 8, L), F32),
            pltpu.SemaphoreType.DMA((2, N, S)),
            pltpu.SemaphoreType.DMA((2, N, S)),
            pltpu.SemaphoreType.DMA((S,)),
            pltpu.SemaphoreType.DMA((S,)),
            pltpu.SemaphoreType.DMA((bands,)),
            pltpu.SemaphoreType.DMA((bands,)),
        ],
        compiler_params=pltpu.CompilerParams(
            collective_id=0, has_side_effects=True, vmem_limit_bytes=56 * 1024 * 1024
        ),
    )(
        positions.T,
        proj_atom,
        proj_chan,
        coupling,
        occupations,
        orbitals.reshape(N * cols, wide),
        cutoff_mask.reshape(cols, length),
        ix,
        channels.reshape(C, cols, length),
        tz,
        t2,
        potential,
        f2,
        tb,
        fx,
    )
    pieces = 4
    applied, density = pl.pallas_call(
        functools.partial(hand_on, pieces),
        out_shape=(
            jax.ShapeDtypeStruct((N * cols, wide), BF16),
            jax.ShapeDtypeStruct(potential.shape, F32),
        ),
        in_specs=[hbm] * 2,
        out_specs=(hbm, hbm),
        scratch_shapes=[
            pltpu.VMEM((N * cols, wide), BF16),
            pltpu.VMEM(potential.shape, F32),
            pltpu.SemaphoreType.DMA((2, pieces)),
            pltpu.SemaphoreType.DMA((2, pieces)),
        ],
    )(applied, density)
    return (applied.reshape(orbitals.shape), density)


def solution(mesh):
    placed = (
        P("band", "gy", "gz", None),
        P(("gy", "gz"), None, None),
        P("gy", "gz", None),
        P(None, "gy", "gz", None),
        P(),
        P(),
        P(),
        P(),
        P("band"),
    )
    return jax.shard_map(
        shards,
        mesh=mesh,
        in_specs=placed,
        out_specs=(P("band", "gy", "gz", None), P(("gy", "gz"), None, None)),
        check_vma=False,
    )
```

```python
import functools
import math

import jax
import jax.numpy as jnp
import ml_dtypes
import numpy as np
from jax import lax
from jax.experimental import pallas as pl
from jax.experimental.pallas import tpu as pltpu
from jax.sharding import PartitionSpec as P

kinetic_scale = 1.0 / 1024.0
MESH = pl.DeviceIdType.MESH
F32 = jnp.float32
BF16 = jnp.bfloat16


def dot(a, b, dims):
    return lax.dot_general(a, b, (dims, ((), ())), preferred_element_type=F32)


def parts_of(length, sign_value):
    index = np.arange(length)
    angle = 2.0 * np.pi / length * (index[:, None] * index[None, :] % length)
    cosine = np.cos(angle) / math.sqrt(length)
    sine = sign_value * np.sin(angle) / math.sqrt(length)
    return cosine, sine


def tables(length, rows_z, parts_z):
    group = length // rows_z
    same = np.eye(group)
    out = []
    for sign in (1.0, -1.0):
        c, s = parts_of(length, sign)
        square = np.block([[c, -s], [s, c]])
        out.append(square)
    inv_sq, fwd_sq = out
    order = np.arange(2 * length).reshape(2, length // 8, 8).transpose(1, 0, 2).reshape(-1)
    inv_x = inv_sq[order]
    fwd_x = fwd_sq.T[order]
    c, s = parts_of(length, 1.0)
    z_in = [
        np.einsum("wqz,jk->qjzkw", t.reshape(length, parts_z, rows_z), same).reshape(
            parts_z * group * rows_z, group * length
        )
        for t in (c, s)
    ]
    c, s = parts_of(length, -1.0)
    z_out = [
        np.einsum("qzw,jk->jwqkz", t.reshape(parts_z, rows_z, length), same).reshape(
            group * length, parts_z * group * rows_z
        )
        for t in (c, s)
    ]
    made = (inv_x, np.concatenate(z_in, 1), inv_sq, fwd_sq, np.concatenate(z_out, 1), fwd_x)
    return [np.asarray(t, dtype=np.float32).astype(ml_dtypes.bfloat16) for t in made]


def folds(length, rows):
    group = length // rows
    count = rows // group
    first = np.arange(rows) + length // 4
    inside = first[:, None] ** 2 + first[None, :] ** 2 < (length // 2) ** 2
    width = inside.reshape(count, group, rows).any(axis=1).sum(axis=1)
    kept = [g for g in range(count) if width[g]]
    plan = []
    while kept:
        g = kept.pop(0)
        other = None
        for h in reversed(kept):
            if width[g] + width[h] <= rows:
                other = h
                kept.remove(h)
                break
        plan.append((g, other, int(width[g])))
    dropped = [g for g in range(count) if not width[g]]
    return plan, dropped


def kernel(
    sizes,
    pos_ref,
    atom_ref,
    kind_ref,
    coup_ref,
    occ_ref,
    orb_hbm,
    mask_hbm,
    ix_hbm,
    chan_hbm,
    tz_hbm,
    t2_hbm,
    pot_hbm,
    f2_hbm,
    tb_hbm,
    fx_hbm,
    out_hbm,
    dens_hbm,
    orb_ref,
    mask_ref,
    ix_ref,
    chan_ref,
    tz_ref,
    t2_ref,
    pot_ref,
    f2_ref,
    tb_ref,
    fx_ref,
    out_ref,
    dens_out_ref,
    in_sem,
    out_sem,
    masked,
    tx,
    rx,
    tx2,
    rx2,
    txc,
    rxc,
    txc2,
    rxc2,
    zs,
    dens,
    dens_rx,
    extra,
    phase,
    fold,
    foldt,
    weighed,
    over_tx,
    over_rx,
    send_sem,
    recv_sem,
    over_send,
    over_recv,
    dens_send,
    dens_recv,
):
    N, C, A, length, rows_y, rows_z, py, pz, bands = sizes
    L = 2 * C * N * A
    half = L // 2
    group = length // rows_z
    G = rows_y // group
    S = py * pz
    cols = rows_y * rows_z
    gy = lax.axis_index("gy")
    gz = lax.axis_index("gz")
    band = lax.axis_index("band")
    me = gy * pz + gz

    half_rows = cols
    moves = [
        pltpu.make_async_copy(
            orb_hbm.at[pl.ds(n * half_rows, half_rows)],
            orb_ref.at[pl.ds(n * half_rows, half_rows)],
            in_sem.at[n],
        )
        for n in range(N)
    ]
    held = (
        (ix_hbm, ix_ref),
        (mask_hbm, mask_ref),
        (chan_hbm, chan_ref),
        (tz_hbm, tz_ref),
        (t2_hbm, t2_ref),
        (pot_hbm, pot_ref),
        (f2_hbm, f2_ref),
        (tb_hbm, tb_ref),
        (fx_hbm, fx_ref),
    )
    loads = [pltpu.make_async_copy(a, b, in_sem.at[N + i]) for i, (a, b) in enumerate(held)]
    for move in loads[:2] + moves:
        move.start()

    def peer(d):
        to = lax.rem(me + d, S)
        return to, {"gy": to // pz, "gz": lax.rem(to, pz)}

    def place_of(to_y, to_z):
        return to_y * pz + to_z, {"gy": to_y, "gz": to_z}

    if pz == 4:
        far = [lax.rem(gz + 2, pz), 3 - gz, gz + 1 - 2 * lax.rem(gz, 2)]
    else:
        far = [lax.rem(gz + k, pz) for k in range(1, pz)]

    barrier = pltpu.get_barrier_semaphore()

    def greet(d, c):
        pl.semaphore_signal(barrier, inc=1, device_id=peer(d)[1], device_id_type=MESH)
        return c

    def greet_band(d, c):
        pl.semaphore_signal(
            barrier, inc=1, device_id={"band": lax.rem(band + d, bands)}, device_id_type=MESH
        )
        return c

    lax.fori_loop(1, S, greet, 0)
    lax.fori_loop(1, bands, greet_band, 0)

    plan, dropped = folds(length, rows_y)
    corner = [k for k in range(pz) if 0 < k < pz - 1]

    def middle(k, parts):
        return (k > 0) & (k < parts - 1)

    def is_corner(y, z):
        return middle(y, py) & middle(z, pz)

    def place_in(t, y):
        return jnp.where(y >= py // 2, G - 1 - t, t)

    def shifted(block, amount, flip):
        return pltpu.roll(block, (128 - amount) % 128 if flip else amount % 128, 1)

    def depth_in(shape, flip):
        z = lax.rem(lax.broadcasted_iota(jnp.int32, shape, 1), rows_z)
        return rows_z - 1 - z if flip else z

    wide_bufs = ((tx, rx), (tx2, rx2))
    slim_bufs = ((txc, rxc), (txc2, rxc2))

    def block_copy(slim, step, n, to, place, slot):
        src, dst = (slim_bufs if slim else wide_bufs)[step]
        return pltpu.make_async_remote_copy(
            src_ref=src.at[to, n],
            dst_ref=dst.at[slot, n],
            send_sem=send_sem.at[step, n, to],
            recv_sem=recv_sem.at[step, n, slot],
            device_id=place,
            device_id_type=MESH,
        )

    def by_kind(slim, act):
        pl.when(slim)(lambda: act(True))
        pl.when(jnp.logical_not(slim))(lambda: act(False))

    def send_row(step, n, d):
        to_y = lax.rem(gy + d, py)
        for to_z in far + [gz]:
            to, place = place_of(to_y, to_z)
            slim = is_corner(gy, gz) if step == 0 else is_corner(to_y, to_z)

            def start():
                by_kind(slim, lambda k: block_copy(k, step, n, to, place, me).start())

            if to_z is gz:
                pl.when(d > 0)(start)
            else:
                start()

    def wait_row(step, n, d):
        from_y = lax.rem(gy + py - d, py)
        for from_z in far + [gz]:
            frm, place = place_of(from_y, from_z)
            slim = is_corner(from_y, from_z) if step == 0 else is_corner(gy, gz)

            def wait():
                by_kind(slim, lambda k: block_copy(k, step, n, frm, place, frm).wait_recv())

            if from_z is gz:
                pl.when(d > 0)(wait)
            else:
                wait()

    def wait_sent(step, n):
        def one(d, c):
            to, place = peer(d)
            to_y, to_z = place["gy"], place["gz"]
            slim = is_corner(gy, gz) if step == 0 else is_corner(to_y, to_z)
            by_kind(slim, lambda k: block_copy(k, step, n, to, place, me).wait_send())
            return c

        lax.fori_loop(1, S, one, 0)

    def fold_mine(n):
        for t, (g, other, width) in enumerate(plan):
            block = tx[:, n, place_in(g, gy)].astype(F32).reshape(S * 16, 128)
            if other is not None:
                more = tx[:, n, place_in(other, gy)].astype(F32).reshape(S * 16, 128)
                block = block + jnp.where(
                    gz >= pz // 2, shifted(more, width, True), shifted(more, width, False)
                )
            txc[:, n, t] = block.astype(BF16).reshape(S, 16, 128)

    def unfold_from(n, y, k):
        s = y * pz + k
        flip = k >= pz // 2
        depth = depth_in((16, 128), flip)
        for t, (g, other, width) in enumerate(plan):
            block = rxc[s, n, t].astype(F32)
            if other is None:
                rx[s, n, place_in(g, y)] = block.astype(BF16)
            else:
                rx[s, n, place_in(g, y)] = jnp.where(depth < width, block, 0.0).astype(BF16)
                more = shifted(block, width, not flip)
                more = jnp.where(depth < rows_z - width, more, 0.0)
                rx[s, n, place_in(other, y)] = more.astype(BF16)
        for g in dropped:
            rx[s, n, place_in(g, y)] = jnp.zeros((16, 128), BF16)

    def fold_for(n, y, k):
        s = y * pz + k
        flip = k >= pz // 2
        depth = depth_in((16, 128), flip)
        for t, (g, other, width) in enumerate(plan):
            block = tx2[s, n, place_in(g, y)].astype(F32)
            if other is not None:
                more = shifted(tx2[s, n, place_in(other, y)].astype(F32), width, flip)
                block = jnp.where(depth < width, block, more)
            txc2[s, n, t] = block.astype(BF16)

    def unfold_mine(n):
        for t, (g, other, width) in enumerate(plan):
            block = rxc2[:, n, t]
            rx2[:, n, place_in(g, gy)] = block
            if other is not None:
                block = block.astype(F32).reshape(S * 16, 128)
                more = jnp.where(
                    gz >= pz // 2, shifted(block, width, False), shifted(block, width, True)
                )
                rx2[:, n, place_in(other, gy)] = more.astype(BF16).reshape(S, 16, 128)
        for g in dropped:
            rx2[:, n, place_in(g, gy)] = jnp.zeros((S, 16, 128), BF16)

    def x_group(n, h, c):
        rows = pl.ds(pl.multiple_of(n * cols + h * 256, 256), 256)
        keep = mask_ref[pl.ds(pl.multiple_of(h * 256, 256), 256), :] != 0
        for part in range(2):
            span = pl.ds(part * length, length)
            block = jnp.where(keep, orb_ref[rows, span].astype(F32), 0.0)
            masked[rows, span] = block.astype(BF16)
        made = dot(ix_ref[...], masked[rows, :], ((1,), (1,))).astype(BF16)
        tx[:, n, 2 * h] = made[:, :128].reshape(S, 16, 128)
        tx[:, n, 2 * h + 1] = made[:, 128:].reshape(S, 16, 128)
        return c

    loads[0].wait()
    loads[1].wait()
    def send_first(n):
        pl.when(is_corner(gy, gz))(functools.partial(fold_mine, n))

        def send_all(d, c):
            send_row(0, n, d)
            return c

        lax.fori_loop(0, py, send_all, 0)
        rx[me, n] = tx[me, n]

    for n in range(N):
        moves[n].wait()
        lax.fori_loop(0, G // 2, functools.partial(x_group, n), 0)
        if n == 0:
            pl.semaphore_wait(barrier, S - 1 + bands - 1)
            send_first(0)
            for move in loads[2:]:
                move.start()

    def centred(index):
        return jnp.where(index >= length // 2, index - length, index).astype(F32)

    def turn(amount):
        quarter = jnp.round(amount * 4.0)
        rest = (2.0 * math.pi) * (amount - 0.25 * quarter)
        sq = rest * rest
        cosine = 1.0 + sq * (
            -0.5 + sq * (1.0 / 24 + sq * (-1.0 / 720 + sq * (1.0 / 40320 - sq * (1.0 / 3628800))))
        )
        sine = rest * (
            1.0
            + sq * (-1.0 / 6 + sq * (1.0 / 120 + sq * (-1.0 / 5040 + sq * (1.0 / 362880))))
        )
        left = quarter - 4.0 * jnp.floor(quarter * 0.25)
        odd = (left == 1.0) | (left == 3.0)
        first = jnp.where(odd, sine, cosine)
        second = jnp.where(odd, cosine, sine)
        first = jnp.where((left == 1.0) | (left == 2.0), -first, first)
        second = jnp.where(left >= 2.0, -second, second)
        return first, second

    fy = centred(lax.broadcasted_iota(jnp.int32, (rows_y, L), 0) + gy * rows_y)
    fz = centred(lax.broadcasted_iota(jnp.int32, (rows_z, L), 0) + gz * rows_z)
    fx = centred(lax.broadcasted_iota(jnp.int32, (L, length), 1))
    lane = lax.broadcasted_iota(jnp.int32, (1, L), 1)
    lane_atom = lax.rem(lane, A)
    lane_chan = lax.rem(lane, half) // (N * A)
    row_atom = lax.rem(lax.broadcasted_iota(jnp.int32, (L, length), 0), A)
    at_x = jnp.zeros((L, length), F32)
    at_y = jnp.zeros((1, L), F32)
    at_z = jnp.zeros((1, L), F32)
    for a in range(A):
        at_x = jnp.where(row_atom == a, pos_ref[0, a], at_x)
        at_y = jnp.where(lane_atom == a, pos_ref[1, a], at_y)
        at_z = jnp.where(lane_atom == a, pos_ref[2, a], at_z)
    cy, sy = turn(fy * at_y)
    cz, sz = turn(fz * at_z)
    cx, sx = turn(fx * at_x)
    for y in range(rows_y):
        at = pl.ds(y * rows_z, rows_z)
        phase[0, at, :] = cy[y : y + 1] * cz - sy[y : y + 1] * sz
        phase[1, at, :] = sy[y : y + 1] * cz + cy[y : y + 1] * sz
    row = lax.broadcasted_iota(jnp.int32, (L, length), 0)
    pair = lax.rem(row, half) // A
    waves = (jnp.where(row < half, cx, sx), jnp.where(row < half, -sx, cx))
    lane_pair = lax.rem(lax.broadcasted_iota(jnp.int32, (length, L), 1), half) // A
    for part in range(2):
        turned = waves[part].T
        for i in range(C * N):
            at = i * 2 * length + part * length
            fold[:, pl.ds(at, length)] = jnp.where(pair == i, waves[part], 0.0).astype(BF16)
            foldt[pl.ds(at, length), :] = jnp.where(lane_pair == i, turned, 0.0).astype(BF16)
    sign = jnp.where(lane < half, -1.0, 1.0)

    loads[2].wait()

    def over_group(h, total):
        at = pl.ds(pl.multiple_of(h * 256, 256), 256)
        for c in range(C):
            profile = chan_ref[c, at, :]
            for n in range(N):
                rows = pl.ds(pl.multiple_of(n * cols + h * 256, 256), 256)
                for part in range(2):
                    lanes = pl.ds(((c * N + n) * 2 + part) * length, length)
                    weighed[:, lanes] = profile * masked[rows, pl.ds(part * length, length)]
        found = dot(weighed[...], foldt[...], ((1,), (0,)))
        swapped = pltpu.roll(found, half, 1)
        value = phase[0, at, :] * found + sign * (phase[1, at, :] * swapped)
        return total + jnp.sum(value, axis=0, keepdims=True)

    total = lax.fori_loop(0, G // 2, over_group, jnp.zeros((1, L), F32))
    over_tx[...] = jnp.broadcast_to(total, (8, L))

    def over_copy(to, place, slot):
        return pltpu.make_async_remote_copy(
            src_ref=over_tx,
            dst_ref=over_rx.at[slot],
            send_sem=over_send.at[to],
            recv_sem=over_recv.at[slot],
            device_id=place,
            device_id_type=MESH,
        )

    def over_start(d, c):
        to, place = peer(d)
        over_copy(to, place, me).start()
        return c

    lax.fori_loop(1, S, over_start, 0)
    over_rx[me] = over_tx[...]

    if N > 1:
        send_first(1)

    for move in loads[3:]:
        move.wait()
    for n in range(N):

        def z_in(d, c):
            wait_row(0, n, d)
            q = lax.rem(gy + py - d, py)
            for k in corner:
                pl.when(middle(q, py) & (q * pz + k != me))(
                    functools.partial(unfold_from, n, q, k)
                )
            lhs = jnp.concatenate(
                [rx[q * pz + k, n].reshape(G * 16, 128) for k in range(pz)], axis=1
            )
            made = dot(lhs, tz_ref[...], ((1,), (0,)))
            u = made[:, : group * length].reshape(G, 2, 8, group * length)
            v = made[:, group * length :].reshape(G, 2, 8, group * length)
            re = u[:, 0] - v[:, 1]
            im = v[:, 0] + u[:, 1]
            for g in range(G):
                for j in range(group):
                    at = pl.multiple_of((q * rows_y + g * group + j) * 16, 16)
                    zs[pl.ds(at, 8), :] = re[g, :, j * length : (j + 1) * length]
                    zs[pl.ds(at + 8, 8), :] = im[g, :, j * length : (j + 1) * length]
            return c

        lax.fori_loop(0, py, z_in, 0)
        for x in range(0, 8, 2):
            spans = [pl.ds(x + i, length, stride=16) for i in (0, 1, 8, 9)]
            got = [zs[span, :] for span in spans]
            both = jnp.concatenate(
                [jnp.concatenate(got[:2], axis=1), jnp.concatenate(got[2:], axis=1)], axis=0
            ).astype(BF16)
            field = dot(t2_ref[...], both, ((1,), (0,)))
            ends = []
            for i in range(2):
                lanes = slice(i * length, (i + 1) * length)
                re, im = field[:length, lanes], field[length:, lanes]
                weight = occ_ref[n] * (re * re + im * im)
                dens[x + i] = weight if n == 0 else dens[x + i] + weight
                pot = pot_ref[x + i]
                ends.append(jnp.concatenate([pot * re, pot * im], axis=0).astype(BF16))
            back = dot(f2_ref[...], jnp.concatenate(ends, axis=1), ((1,), (0,)))
            zs[spans[0], :] = back[:length, :length]
            zs[spans[1], :] = back[:length, length:]
            zs[spans[2], :] = back[length:, :length]
            zs[spans[3], :] = back[length:, length:]

        def z_out(d, c):
            q = lax.rem(gy + d, py)
            at = pl.ds(pl.multiple_of(q * rows_y * 16, 512), rows_y * 16)
            block = zs[at, :].reshape(G, group, 16, length)
            lhs = jnp.concatenate(
                [block[:, j].reshape(G * 16, length) for j in range(group)], axis=1
            ).astype(BF16)
            made = dot(lhs, tb_ref[...], ((1,), (0,)))
            u = made[:, : pz * 128].reshape(G, 2, 8, pz * 128)
            v = made[:, pz * 128 :].reshape(G, 2, 8, pz * 128)
            re = u[:, 0] - v[:, 1]
            im = v[:, 0] + u[:, 1]
            joined = jnp.concatenate([re, im], axis=1).astype(BF16)
            for k in range(pz):
                tx2[q * pz + k, n] = joined[:, :, k * 128 : (k + 1) * 128]
            for k in corner:
                pl.when(middle(q, py))(functools.partial(fold_for, n, q, k))
            send_row(1, n, d)
            return c

        lax.fori_loop(0, py, z_out, 0)

        @pl.when(is_corner(gy, gz))
        def _():
            rxc2[me, n] = txc2[me, n]

        @pl.when(jnp.logical_not(is_corner(gy, gz)))
        def _():
            rx2[me, n] = tx2[me, n]

        if n + 2 < N:
            send_first(n + 2)

    dens_rx[band] = dens[...].astype(BF16)

    def dens_copy(d, slot):
        to = lax.rem(band + d, bands)
        return pltpu.make_async_remote_copy(
            src_ref=dens_rx.at[band],
            dst_ref=dens_rx.at[slot],
            send_sem=dens_send.at[to],
            recv_sem=dens_recv.at[slot],
            device_id={"band": to},
            device_id_type=MESH,
        )

    def dens_start(d, c):
        dens_copy(d, band).start()
        return c

    lax.fori_loop(1, bands, dens_start, 0)

    def over_wait(d, c):
        frm, place = peer(d)
        over_copy(frm, place, frm).wait_recv()
        return c

    lax.fori_loop(1, S, over_wait, 0)
    meet = over_rx[0]
    for s in range(1, S):
        meet = meet + over_rx[s]
    meet = meet[0:1]
    coef = jnp.zeros((1, L), F32)
    for p in range(coup_ref.shape[0]):
        hit = (lane_chan == kind_ref[p]) & (lane_atom == atom_ref[p])
        coef = coef + jnp.where(hit, (coup_ref[p] * meet).astype(BF16).astype(F32), 0.0)
    coef_swapped = pltpu.roll(jnp.broadcast_to(coef, (8, L)), half, 1)[0:1]

    def apply_group(h, c):
        at = pl.ds(pl.multiple_of(h * 256, 256), 256)
        lhs = phase[0, at, :] * coef - phase[1, at, :] * (sign * coef_swapped)
        lhs = lhs.astype(BF16)
        index = lax.broadcasted_iota(jnp.int32, (256, length), 0) + h * 256
        ky = centred(gy * rows_y + index // rows_z)
        kz = centred(gz * rows_z + lax.rem(index, rows_z))
        kx = centred(lax.broadcasted_iota(jnp.int32, (256, length), 1))
        energy = (kinetic_scale * 0.5) * (ky * ky + kz * kz + kx * kx)
        for n in range(N):
            rows = pl.ds(pl.multiple_of(n * cols + h * 256, 256), 256)
            parts = [
                energy * masked[rows, pl.ds(part * length, length)].astype(F32)
                for part in range(2)
            ]
            for k in range(C):
                profile = chan_ref[k, at, :].astype(F32)
                made = dot(
                    lhs, fold[:, pl.ds((k * N + n) * 2 * length, 2 * length)], ((1,), (0,))
                )
                parts[0] = parts[0] + profile * made[:, :length]
                parts[1] = parts[1] + profile * made[:, length:]
            for part in range(2):
                extra[rows, pl.ds(part * length, length)] = parts[part]
        return c

    lax.fori_loop(0, G // 2, apply_group, 0)

    def dens_wait(d, c):
        dens_copy(d, lax.rem(band + d, bands)).wait_recv()
        return c

    lax.fori_loop(1, bands, dens_wait, 0)
    whole = dens_rx[0].astype(F32)
    for b in range(1, bands):
        whole = whole + dens_rx[b].astype(F32)
    dens_out_ref[...] = whole
    dens_move = pltpu.make_async_copy(dens_out_ref, dens_hbm, out_sem.at[N])
    dens_move.start()

    def over_done(d, c):
        to, place = peer(d)
        over_copy(to, place, me).wait_send()
        return c

    lax.fori_loop(1, S, over_done, 0)

    def dens_done(d, c):
        dens_copy(d, band).wait_send()
        return c

    lax.fori_loop(1, bands, dens_done, 0)
    leaves = []
    for n in range(N):
        wait_sent(0, n)
    for n in range(N):
        wait_sent(1, n)

        def arrive(d, c):
            wait_row(1, n, d)
            return c

        lax.fori_loop(0, py, arrive, 0)
        pl.when(is_corner(gy, gz))(functools.partial(unfold_mine, n))

        def finish(h, c):
            rows = pl.ds(pl.multiple_of(n * cols + h * 256, 256), 256)
            keep = mask_ref[pl.ds(pl.multiple_of(h * 256, 256), 256), :] != 0
            block = jnp.concatenate(
                [rx2[:, n, 2 * h + i].reshape(S * 16, 128) for i in range(2)], axis=1
            )
            local = dot(block, fx_ref[...], ((0,), (0,)))
            for part in range(2):
                lanes = pl.ds(part * length, length)
                value = local[:, part * length : (part + 1) * length] + extra[rows, lanes]
                out_ref[rows, lanes] = jnp.where(keep, value, 0.0).astype(BF16)
            return c

        lax.fori_loop(0, G // 2, finish, 0)
        span = pl.ds(n * half_rows, half_rows)
        leave = pltpu.make_async_copy(out_ref.at[span], out_hbm.at[span], out_sem.at[n])
        leave.start()
        leaves.append(leave)

    dens_move.wait()
    for leave in leaves:
        leave.wait()


def hand_on(pieces, *refs):
    ins, outs, held = refs[:2], refs[2:4], refs[4:6]
    sem_in, sem_out = refs[6:]
    steps = []
    for i in range(2):
        rows = ins[i].shape[0] // pieces
        for k in range(pieces):
            span = pl.ds(k * rows, rows)
            here = held[i].at[span]
            steps.append(
                (
                    pltpu.make_async_copy(ins[i].at[span], here, sem_in.at[i, k]),
                    pltpu.make_async_copy(here, outs[i].at[span], sem_out.at[i, k]),
                )
            )
    for read, _ in steps:
        read.start()
    for read, write in steps:
        read.wait()
        write.start()
    for _, write in steps:
        write.wait()


def shards(
    orbitals,
    potential,
    cutoff_mask,
    channels,
    positions,
    proj_atom,
    proj_chan,
    coupling,
    occupations,
):
    N, rows_y, rows_z, wide = orbitals.shape
    length = wide // 2
    C = channels.shape[0]
    A = positions.shape[0]
    py, pz, bands = lax.axis_size("gy"), lax.axis_size("gz"), lax.axis_size("band")
    S = py * pz
    L = 2 * C * N * A
    G = rows_y * rows_z // 128
    cols = rows_y * rows_z
    ix, tz, t2, f2, tb, fx = [jnp.asarray(t) for t in tables(length, rows_z, pz)]
    hbm = pl.BlockSpec(memory_space=pl.ANY)
    smem = pl.BlockSpec(memory_space=pltpu.SMEM)
    sizes = (N, C, A, length, rows_y, rows_z, py, pz, bands)
    planes = (S, N, G, 16, 128)
    slim = (S, N, len(folds(length, rows_y)[0]), 16, 128)
    applied, density = pl.pallas_call(
        functools.partial(kernel, sizes),
        out_shape=(
            jax.ShapeDtypeStruct((N * cols, wide), BF16),
            jax.ShapeDtypeStruct(potential.shape, F32),
        ),
        in_specs=[smem] * 5 + [hbm] * 10,
        out_specs=(hbm, hbm),
        scratch_shapes=[
            pltpu.VMEM((N * cols, wide), BF16),
            pltpu.VMEM((cols, length), jnp.int32),
            pltpu.VMEM(ix.shape, BF16),
            pltpu.VMEM((C, cols, length), BF16),
            pltpu.VMEM(tz.shape, BF16),
            pltpu.VMEM(t2.shape, BF16),
            pltpu.VMEM(potential.shape, F32),
            pltpu.VMEM(f2.shape, BF16),
            pltpu.VMEM(tb.shape, BF16),
            pltpu.VMEM(fx.shape, BF16),
            pltpu.VMEM((N * cols, wide), BF16),
            pltpu.VMEM(potential.shape, F32),
            pltpu.SemaphoreType.DMA((N + 9,)),
            pltpu.SemaphoreType.DMA((N + 1,)),
            pltpu.VMEM((N * cols, wide), BF16),
            pltpu.VMEM(planes, BF16),
            pltpu.VMEM(planes, BF16),
            pltpu.VMEM(planes, BF16),
            pltpu.VMEM(planes, BF16),
            pltpu.VMEM(slim, BF16),
            pltpu.VMEM(slim, BF16),
            pltpu.VMEM(slim, BF16),
            pltpu.VMEM(slim, BF16),
            pltpu.VMEM((length * 16, length), F32),
            pltpu.VMEM(potential.shape, F32),
            pltpu.VMEM((bands,) + potential.shape, BF16),
            pltpu.VMEM((N * cols, wide), F32),
            pltpu.VMEM((2, cols, L), F32),
            pltpu.VMEM((L, C * N * wide), BF16),
            pltpu.VMEM((C * N * wide, L), BF16),
            pltpu.VMEM((256, C * N * wide), BF16),
            pltpu.VMEM((8, L), F32),
            pltpu.VMEM((S, 8, L), F32),
            pltpu.SemaphoreType.DMA((2, N, S)),
            pltpu.SemaphoreType.DMA((2, N, S)),
            pltpu.SemaphoreType.DMA((S,)),
            pltpu.SemaphoreType.DMA((S,)),
            pltpu.SemaphoreType.DMA((bands,)),
            pltpu.SemaphoreType.DMA((bands,)),
        ],
        compiler_params=pltpu.CompilerParams(
            collective_id=0, has_side_effects=True, vmem_limit_bytes=56 * 1024 * 1024
        ),
    )(
        positions.T,
        proj_atom,
        proj_chan,
        coupling,
        occupations,
        orbitals.reshape(N * cols, wide),
        cutoff_mask.reshape(cols, length),
        ix,
        channels.reshape(C, cols, length),
        tz,
        t2,
        potential,
        f2,
        tb,
        fx,
    )
    pieces = 4
    applied, density = pl.pallas_call(
        functools.partial(hand_on, pieces),
        out_shape=(
            jax.ShapeDtypeStruct((N * cols, wide), BF16),
            jax.ShapeDtypeStruct(potential.shape, F32),
        ),
        in_specs=[hbm] * 2,
        out_specs=(hbm, hbm),
        scratch_shapes=[
            pltpu.VMEM((N * cols, wide), BF16),
            pltpu.VMEM(potential.shape, F32),
            pltpu.SemaphoreType.DMA((2, pieces)),
            pltpu.SemaphoreType.DMA((2, pieces)),
        ],
    )(applied, density)
    return (applied.reshape(orbitals.shape), density)


def solution(mesh):
    placed = (
        P("band", "gy", "gz", None),
        P(("gy", "gz"), None, None),
        P("gy", "gz", None),
        P(None, "gy", "gz", None),
        P(),
        P(),
        P(),
        P(),
        P("band"),
    )
    return jax.shard_map(
        shards,
        mesh=mesh,
        in_specs=placed,
        out_specs=(P("band", "gy", "gz", None), P(("gy", "gz"), None, None)),
        check_vma=False,
    )
```

```python
import functools
import math

import jax
import jax.numpy as jnp
import ml_dtypes
import numpy as np
from jax import lax
from jax.experimental import pallas as pl
from jax.experimental.pallas import tpu as pltpu
from jax.sharding import PartitionSpec as P

kinetic_scale = 1.0 / 1024.0
MESH = pl.DeviceIdType.MESH
F32 = jnp.float32
BF16 = jnp.bfloat16


def dot(a, b, dims):
    return lax.dot_general(a, b, (dims, ((), ())), preferred_element_type=F32)


def parts_of(length, sign_value):
    index = np.arange(length)
    angle = 2.0 * np.pi / length * (index[:, None] * index[None, :] % length)
    cosine = np.cos(angle) / math.sqrt(length)
    sine = sign_value * np.sin(angle) / math.sqrt(length)
    return cosine, sine


def tables(length, rows_z, parts_z):
    group = length // rows_z
    same = np.eye(group)
    out = []
    for sign in (1.0, -1.0):
        c, s = parts_of(length, sign)
        square = np.block([[c, -s], [s, c]])
        out.append(square)
    inv_sq, fwd_sq = out
    order = np.arange(2 * length).reshape(2, length // 8, 8).transpose(1, 0, 2).reshape(-1)
    inv_x = inv_sq[order]
    fwd_x = fwd_sq.T[order]
    c, s = parts_of(length, 1.0)
    z_in = [
        np.einsum("wqz,jk->qjzkw", t.reshape(length, parts_z, rows_z), same).reshape(
            parts_z * group * rows_z, group * length
        )
        for t in (c, s)
    ]
    c, s = parts_of(length, -1.0)
    z_out = [
        np.einsum("qzw,jk->jwqkz", t.reshape(parts_z, rows_z, length), same).reshape(
            group * length, parts_z * group * rows_z
        )
        for t in (c, s)
    ]
    z_in, z_out = (
        np.stack([t.reshape(len(t), -1, 128) for t in pair], 2).reshape(len(pair[0]), -1)
        for pair in (z_in, z_out)
    )
    made = (inv_x, z_in, inv_sq, fwd_sq, z_out, fwd_x)
    return [np.asarray(t, dtype=np.float32).astype(ml_dtypes.bfloat16) for t in made]


def folds(length, rows):
    group = length // rows
    count = rows // group
    first = np.arange(rows) + length // 4
    inside = first[:, None] ** 2 + first[None, :] ** 2 < (length // 2) ** 2
    width = inside.reshape(count, group, rows).any(axis=1).sum(axis=1)
    kept = [g for g in range(count) if width[g]]
    plan = []
    while kept:
        g = kept.pop(0)
        other = None
        for h in reversed(kept):
            if width[g] + width[h] <= rows:
                other = h
                kept.remove(h)
                break
        plan.append((g, other, int(width[g])))
    dropped = [g for g in range(count) if not width[g]]
    return plan, dropped


def kernel(
    sizes,
    pos_ref,
    atom_ref,
    kind_ref,
    coup_ref,
    occ_ref,
    orb_hbm,
    mask_hbm,
    ix_hbm,
    chan_hbm,
    tz_hbm,
    t2_hbm,
    pot_hbm,
    f2_hbm,
    tb_hbm,
    fx_hbm,
    out_hbm,
    dens_hbm,
    orb_ref,
    mask_ref,
    ix_ref,
    chan_ref,
    tz_ref,
    t2_ref,
    pot_ref,
    f2_ref,
    tb_ref,
    fx_ref,
    out_ref,
    dens_out_ref,
    in_sem,
    out_sem,
    masked,
    tx,
    rx,
    tx2,
    rx2,
    txc,
    rxc,
    txc2,
    rxc2,
    zs,
    dens,
    dens_rx,
    extra,
    phase,
    fold,
    foldt,
    weighed,
    stack,
    over_tx,
    over_rx,
    send_sem,
    recv_sem,
    over_send,
    over_recv,
    dens_send,
    dens_recv,
):
    N, C, A, length, rows_y, rows_z, py, pz, bands = sizes
    L = 2 * C * N * A
    half = L // 2
    group = length // rows_z
    G = rows_y // group
    S = py * pz
    cols = rows_y * rows_z
    gy = lax.axis_index("gy")
    gz = lax.axis_index("gz")
    band = lax.axis_index("band")
    me = gy * pz + gz

    half_rows = cols
    moves = [
        pltpu.make_async_copy(
            orb_hbm.at[pl.ds(n * half_rows, half_rows)],
            orb_ref.at[pl.ds(n * half_rows, half_rows)],
            in_sem.at[n],
        )
        for n in range(N)
    ]
    held = (
        (ix_hbm, ix_ref),
        (mask_hbm, mask_ref),
        (chan_hbm, chan_ref),
        (tz_hbm, tz_ref),
        (t2_hbm, t2_ref),
        (pot_hbm, pot_ref),
        (f2_hbm, f2_ref),
        (tb_hbm, tb_ref),
        (fx_hbm, fx_ref),
    )
    loads = [pltpu.make_async_copy(a, b, in_sem.at[N + i]) for i, (a, b) in enumerate(held)]
    for move in loads[:2] + moves:
        move.start()

    def peer(d):
        to = lax.rem(me + d, S)
        return to, {"gy": to // pz, "gz": lax.rem(to, pz)}

    def place_of(to_y, to_z):
        return to_y * pz + to_z, {"gy": to_y, "gz": to_z}

    if pz == 4:
        far = [lax.rem(gz + 2, pz), 3 - gz, gz + 1 - 2 * lax.rem(gz, 2)]
    else:
        far = [lax.rem(gz + k, pz) for k in range(1, pz)]

    barrier = pltpu.get_barrier_semaphore()

    def greet(d, c):
        pl.semaphore_signal(barrier, inc=1, device_id=peer(d)[1], device_id_type=MESH)
        return c

    def greet_band(d, c):
        pl.semaphore_signal(
            barrier, inc=1, device_id={"band": lax.rem(band + d, bands)}, device_id_type=MESH
        )
        return c

    lax.fori_loop(1, S, greet, 0)
    lax.fori_loop(1, bands, greet_band, 0)

    plan, dropped = folds(length, rows_y)
    corner = [k for k in range(pz) if 0 < k < pz - 1]

    def middle(k, parts):
        return (k > 0) & (k < parts - 1)

    def is_corner(y, z):
        return middle(y, py) & middle(z, pz)

    def place_in(t, y):
        return jnp.where(y >= py // 2, G - 1 - t, t)

    def shifted(block, amount, flip):
        return pltpu.roll(block, (128 - amount) % 128 if flip else amount % 128, 1)

    def depth_in(shape, flip):
        z = lax.rem(lax.broadcasted_iota(jnp.int32, shape, 1), rows_z)
        return rows_z - 1 - z if flip else z

    wide_bufs = ((tx, rx), (tx2, rx2))
    slim_bufs = ((txc, rxc), (txc2, rxc2))

    def block_copy(slim, step, n, to, place, slot):
        src, dst = (slim_bufs if slim else wide_bufs)[step]
        return pltpu.make_async_remote_copy(
            src_ref=src.at[to, n],
            dst_ref=dst.at[slot, n],
            send_sem=send_sem.at[step, n, to],
            recv_sem=recv_sem.at[step, n, slot],
            device_id=place,
            device_id_type=MESH,
        )

    def by_kind(slim, act):
        pl.when(slim)(lambda: act(True))
        pl.when(jnp.logical_not(slim))(lambda: act(False))

    def send_row(step, n, d):
        to_y = lax.rem(gy + d, py)
        for to_z in far + [gz]:
            to, place = place_of(to_y, to_z)
            slim = is_corner(gy, gz) if step == 0 else is_corner(to_y, to_z)

            def start():
                by_kind(slim, lambda k: block_copy(k, step, n, to, place, me).start())

            if to_z is gz:
                pl.when(d > 0)(start)
            else:
                start()

    def wait_row(step, n, d):
        from_y = lax.rem(gy + py - d, py)
        for from_z in far + [gz]:
            frm, place = place_of(from_y, from_z)
            slim = is_corner(from_y, from_z) if step == 0 else is_corner(gy, gz)

            def wait():
                by_kind(slim, lambda k: block_copy(k, step, n, frm, place, frm).wait_recv())

            if from_z is gz:
                pl.when(d > 0)(wait)
            else:
                wait()

    def wait_sent(step, n):
        def one(d, c):
            to, place = peer(d)
            to_y, to_z = place["gy"], place["gz"]
            slim = is_corner(gy, gz) if step == 0 else is_corner(to_y, to_z)
            by_kind(slim, lambda k: block_copy(k, step, n, to, place, me).wait_send())
            return c

        lax.fori_loop(1, S, one, 0)

    def fold_mine(n):
        for t, (g, other, width) in enumerate(plan):
            block = tx[:, n, place_in(g, gy)].astype(F32).reshape(S * 16, 128)
            if other is not None:
                more = tx[:, n, place_in(other, gy)].astype(F32).reshape(S * 16, 128)
                block = block + jnp.where(
                    gz >= pz // 2, shifted(more, width, True), shifted(more, width, False)
                )
            txc[:, n, t] = block.astype(BF16).reshape(S, 16, 128)

    def unfold_from(n, y, k):
        s = y * pz + k
        flip = k >= pz // 2
        depth = depth_in((16, 128), flip)
        for t, (g, other, width) in enumerate(plan):
            block = rxc[s, n, t].astype(F32)
            if other is None:
                rx[s, n, place_in(g, y)] = block.astype(BF16)
            else:
                rx[s, n, place_in(g, y)] = jnp.where(depth < width, block, 0.0).astype(BF16)
                more = shifted(block, width, not flip)
                more = jnp.where(depth < rows_z - width, more, 0.0)
                rx[s, n, place_in(other, y)] = more.astype(BF16)
        for g in dropped:
            rx[s, n, place_in(g, y)] = jnp.zeros((16, 128), BF16)

    def fold_for(n, y, k):
        s = y * pz + k
        flip = k >= pz // 2
        depth = depth_in((16, 128), flip)
        for t, (g, other, width) in enumerate(plan):
            block = tx2[s, n, place_in(g, y)].astype(F32)
            if other is not None:
                more = shifted(tx2[s, n, place_in(other, y)].astype(F32), width, flip)
                block = jnp.where(depth < width, block, more)
            txc2[s, n, t] = block.astype(BF16)

    def unfold_mine(n):
        for t, (g, other, width) in enumerate(plan):
            block = rxc2[:, n, t]
            rx2[:, n, place_in(g, gy)] = block
            if other is not None:
                block = block.astype(F32).reshape(S * 16, 128)
                more = jnp.where(
                    gz >= pz // 2, shifted(block, width, False), shifted(block, width, True)
                )
                rx2[:, n, place_in(other, gy)] = more.astype(BF16).reshape(S, 16, 128)
        for g in dropped:
            rx2[:, n, place_in(g, gy)] = jnp.zeros((S, 16, 128), BF16)

    def x_group(n, h, c):
        rows = pl.ds(pl.multiple_of(n * cols + h * 256, 256), 256)
        keep = mask_ref[pl.ds(pl.multiple_of(h * 256, 256), 256), :] != 0
        for part in range(2):
            span = pl.ds(part * length, length)
            block = jnp.where(keep, orb_ref[rows, span].astype(F32), 0.0)
            masked[rows, span] = block.astype(BF16)
        made = dot(ix_ref[...], masked[rows, :], ((1,), (1,))).astype(BF16)
        tx[:, n, 2 * h] = made[:, :128].reshape(S, 16, 128)
        tx[:, n, 2 * h + 1] = made[:, 128:].reshape(S, 16, 128)
        return c

    loads[0].wait()
    loads[1].wait()
    def send_first(n):
        pl.when(is_corner(gy, gz))(functools.partial(fold_mine, n))

        def send_all(d, c):
            send_row(0, n, d)
            return c

        lax.fori_loop(0, py, send_all, 0)
        rx[me, n] = tx[me, n]

    for n in range(N):
        moves[n].wait()
        lax.fori_loop(0, G // 2, functools.partial(x_group, n), 0)
        if n == 0:
            pl.semaphore_wait(barrier, S - 1 + bands - 1)
            send_first(0)
            for move in loads[2:]:
                move.start()

    def centred(index):
        return jnp.where(index >= length // 2, index - length, index).astype(F32)

    def turn(amount):
        quarter = jnp.round(amount * 4.0)
        rest = (2.0 * math.pi) * (amount - 0.25 * quarter)
        sq = rest * rest
        cosine = 1.0 + sq * (
            -0.5 + sq * (1.0 / 24 + sq * (-1.0 / 720 + sq * (1.0 / 40320 - sq * (1.0 / 3628800))))
        )
        sine = rest * (
            1.0
            + sq * (-1.0 / 6 + sq * (1.0 / 120 + sq * (-1.0 / 5040 + sq * (1.0 / 362880))))
        )
        left = quarter - 4.0 * jnp.floor(quarter * 0.25)
        odd = (left == 1.0) | (left == 3.0)
        first = jnp.where(odd, sine, cosine)
        second = jnp.where(odd, cosine, sine)
        first = jnp.where((left == 1.0) | (left == 2.0), -first, first)
        second = jnp.where(left >= 2.0, -second, second)
        return first, second

    fy = centred(lax.broadcasted_iota(jnp.int32, (rows_y, L), 0) + gy * rows_y)
    fz = centred(lax.broadcasted_iota(jnp.int32, (rows_z, L), 0) + gz * rows_z)
    fx = centred(lax.broadcasted_iota(jnp.int32, (L, length), 1))
    lane = lax.broadcasted_iota(jnp.int32, (1, L), 1)
    lane_atom = lax.rem(lane, A)
    lane_chan = lax.rem(lane, half) // (N * A)
    row_atom = lax.rem(lax.broadcasted_iota(jnp.int32, (L, length), 0), A)
    at_x = jnp.zeros((L, length), F32)
    at_y = jnp.zeros((1, L), F32)
    at_z = jnp.zeros((1, L), F32)
    for a in range(A):
        at_x = jnp.where(row_atom == a, pos_ref[0, a], at_x)
        at_y = jnp.where(lane_atom == a, pos_ref[1, a], at_y)
        at_z = jnp.where(lane_atom == a, pos_ref[2, a], at_z)
    cy, sy = turn(fy * at_y)
    cz, sz = turn(fz * at_z)
    cx, sx = turn(fx * at_x)
    for y in range(rows_y):
        at = pl.ds(y * rows_z, rows_z)
        phase[0, at, :] = cy[y : y + 1] * cz - sy[y : y + 1] * sz
        phase[1, at, :] = sy[y : y + 1] * cz + cy[y : y + 1] * sz
    row = lax.broadcasted_iota(jnp.int32, (L, length), 0)
    pair = lax.rem(row, half) // A
    waves = (jnp.where(row < half, cx, sx), jnp.where(row < half, -sx, cx))
    lane_pair = lax.rem(lax.broadcasted_iota(jnp.int32, (length, L), 1), half) // A
    for part in range(2):
        turned = waves[part].T
        for i in range(C * N):
            at = i * 2 * length + part * length
            fold[:, pl.ds(at, length)] = jnp.where(pair == i, waves[part], 0.0).astype(BF16)
            foldt[pl.ds(at, length), :] = jnp.where(lane_pair == i, turned, 0.0).astype(BF16)
    sign = jnp.where(lane < half, -1.0, 1.0)

    loads[2].wait()

    def over_group(h, total):
        at = pl.ds(pl.multiple_of(h * 256, 256), 256)
        for c in range(C):
            profile = chan_ref[c, at, :]
            for n in range(N):
                rows = pl.ds(pl.multiple_of(n * cols + h * 256, 256), 256)
                for part in range(2):
                    lanes = pl.ds(((c * N + n) * 2 + part) * length, length)
                    weighed[:, lanes] = profile * masked[rows, pl.ds(part * length, length)]
        found = dot(weighed[...], foldt[...], ((1,), (0,)))
        swapped = pltpu.roll(found, half, 1)
        value = phase[0, at, :] * found + sign * (phase[1, at, :] * swapped)
        return total + jnp.sum(value, axis=0, keepdims=True)

    total = lax.fori_loop(0, G // 2, over_group, jnp.zeros((1, L), F32))
    over_tx[...] = jnp.broadcast_to(total, (8, L))

    def over_copy(to, place, slot):
        return pltpu.make_async_remote_copy(
            src_ref=over_tx,
            dst_ref=over_rx.at[slot],
            send_sem=over_send.at[to],
            recv_sem=over_recv.at[slot],
            device_id=place,
            device_id_type=MESH,
        )

    def over_start(d, c):
        to, place = peer(d)
        over_copy(to, place, me).start()
        return c

    lax.fori_loop(1, S, over_start, 0)
    over_rx[me] = over_tx[...]

    if N > 1:
        send_first(1)

    for move in loads[3:]:
        move.wait()
    for n in range(N):

        def z_in(d, c):
            wait_row(0, n, d)
            q = lax.rem(gy + py - d, py)
            for k in corner:
                pl.when(middle(q, py) & (q * pz + k != me))(
                    functools.partial(unfold_from, n, q, k)
                )
            return c

        lax.fori_loop(0, py, z_in, 0)
        for q in range(py):
            for k in range(pz):
                stack[pl.ds(q * G * 16, G * 16), pl.ds(k * 128, 128)] = rx[
                    q * pz + k, n
                ].reshape(G * 16, 128)
        for j in range(group):
            made = dot(stack[...], tz_ref[:, pl.ds(j * 256, 256)], ((1,), (0,)))
            made = made.reshape(py * G, 2, 8, 256)
            re = made[:, 0, :, :128] - made[:, 1, :, 128:]
            im = made[:, 0, :, 128:] + made[:, 1, :, :128]
            for i in range(py * G):
                at = (i * group + j) * 16
                zs[pl.ds(at, 8), :] = re[i]
                zs[pl.ds(at + 8, 8), :] = im[i]
        for x in range(0, 8, 2):
            spans = [pl.ds(x + i, length, stride=16) for i in (0, 1, 8, 9)]
            got = [zs[span, :] for span in spans]
            both = jnp.concatenate(
                [jnp.concatenate(got[:2], axis=1), jnp.concatenate(got[2:], axis=1)], axis=0
            ).astype(BF16)
            field = dot(t2_ref[...], both, ((1,), (0,)))
            ends = []
            for i in range(2):
                lanes = slice(i * length, (i + 1) * length)
                re, im = field[:length, lanes], field[length:, lanes]
                weight = occ_ref[n] * (re * re + im * im)
                dens[x + i] = weight if n == 0 else dens[x + i] + weight
                pot = pot_ref[x + i]
                ends.append(jnp.concatenate([pot * re, pot * im], axis=0).astype(BF16))
            back = dot(f2_ref[...], jnp.concatenate(ends, axis=1), ((1,), (0,)))
            zs[spans[0], :] = back[:length, :length]
            zs[spans[1], :] = back[:length, length:]
            zs[spans[2], :] = back[length:, :length]
            zs[spans[3], :] = back[length:, length:]

        block = zs[...].reshape(py * G, group, 16, length)
        for j in range(group):
            stack[:, pl.ds(j * 128, 128)] = (
                block[:, j].reshape(py * G * 16, length).astype(BF16)
            )
        for k in far + [gz]:
            span = pl.ds(pl.multiple_of(k * 256, 256), 256)
            made = dot(stack[...], tb_ref[:, span], ((1,), (0,)))
            made = made.reshape(py * G, 2, 8, 256)
            re = made[:, 0, :, :128] - made[:, 1, :, 128:]
            im = made[:, 0, :, 128:] + made[:, 1, :, :128]
            joined = jnp.concatenate([re, im], axis=1).astype(BF16).reshape(py, G, 16, 128)
            for q in range(py):
                tx2[q * pz + k, n] = joined[q]
            for fixed in corner:

                @pl.when(k == fixed)
                def _():
                    for q in range(1, py - 1):
                        fold_for(n, q, fixed)

            def send_on(d, c):
                to_y = lax.rem(gy + d, py)
                to, place = place_of(to_y, k)
                by_kind(
                    is_corner(to_y, k),
                    lambda kind: block_copy(kind, 1, n, to, place, me).start(),
                )
                return c

            lax.fori_loop(1 if k is gz else 0, py, send_on, 0)

        @pl.when(is_corner(gy, gz))
        def _():
            rxc2[me, n] = txc2[me, n]

        @pl.when(jnp.logical_not(is_corner(gy, gz)))
        def _():
            rx2[me, n] = tx2[me, n]

        if n + 2 < N:
            send_first(n + 2)

    dens_rx[band] = dens[...].astype(BF16)

    def dens_copy(d, slot):
        to = lax.rem(band + d, bands)
        return pltpu.make_async_remote_copy(
            src_ref=dens_rx.at[band],
            dst_ref=dens_rx.at[slot],
            send_sem=dens_send.at[to],
            recv_sem=dens_recv.at[slot],
            device_id={"band": to},
            device_id_type=MESH,
        )

    def dens_start(d, c):
        dens_copy(d, band).start()
        return c

    lax.fori_loop(1, bands, dens_start, 0)

    def over_wait(d, c):
        frm, place = peer(d)
        over_copy(frm, place, frm).wait_recv()
        return c

    lax.fori_loop(1, S, over_wait, 0)
    meet = over_rx[0]
    for s in range(1, S):
        meet = meet + over_rx[s]
    meet = meet[0:1]
    coef = jnp.zeros((1, L), F32)
    for p in range(coup_ref.shape[0]):
        hit = (lane_chan == kind_ref[p]) & (lane_atom == atom_ref[p])
        coef = coef + jnp.where(hit, (coup_ref[p] * meet).astype(BF16).astype(F32), 0.0)
    coef_swapped = pltpu.roll(jnp.broadcast_to(coef, (8, L)), half, 1)[0:1]

    def apply_group(h, c):
        at = pl.ds(pl.multiple_of(h * 256, 256), 256)
        lhs = phase[0, at, :] * coef - phase[1, at, :] * (sign * coef_swapped)
        lhs = lhs.astype(BF16)
        index = lax.broadcasted_iota(jnp.int32, (256, length), 0) + h * 256
        ky = centred(gy * rows_y + index // rows_z)
        kz = centred(gz * rows_z + lax.rem(index, rows_z))
        kx = centred(lax.broadcasted_iota(jnp.int32, (256, length), 1))
        energy = (kinetic_scale * 0.5) * (ky * ky + kz * kz + kx * kx)
        for n in range(N):
            rows = pl.ds(pl.multiple_of(n * cols + h * 256, 256), 256)
            parts = [
                energy * masked[rows, pl.ds(part * length, length)].astype(F32)
                for part in range(2)
            ]
            for k in range(C):
                profile = chan_ref[k, at, :].astype(F32)
                made = dot(
                    lhs, fold[:, pl.ds((k * N + n) * 2 * length, 2 * length)], ((1,), (0,))
                )
                parts[0] = parts[0] + profile * made[:, :length]
                parts[1] = parts[1] + profile * made[:, length:]
            for part in range(2):
                extra[rows, pl.ds(part * length, length)] = parts[part]
        return c

    lax.fori_loop(0, G // 2, apply_group, 0)

    def dens_wait(d, c):
        dens_copy(d, lax.rem(band + d, bands)).wait_recv()
        return c

    lax.fori_loop(1, bands, dens_wait, 0)
    whole = dens_rx[0].astype(F32)
    for b in range(1, bands):
        whole = whole + dens_rx[b].astype(F32)
    dens_out_ref[...] = whole
    dens_move = pltpu.make_async_copy(dens_out_ref, dens_hbm, out_sem.at[N])
    dens_move.start()

    def over_done(d, c):
        to, place = peer(d)
        over_copy(to, place, me).wait_send()
        return c

    lax.fori_loop(1, S, over_done, 0)

    def dens_done(d, c):
        dens_copy(d, band).wait_send()
        return c

    lax.fori_loop(1, bands, dens_done, 0)
    leaves = []
    for n in range(N):
        wait_sent(0, n)
    for n in range(N):
        wait_sent(1, n)

        def arrive(d, c):
            wait_row(1, n, d)
            return c

        lax.fori_loop(0, py, arrive, 0)
        pl.when(is_corner(gy, gz))(functools.partial(unfold_mine, n))

        def finish(h, c):
            rows = pl.ds(pl.multiple_of(n * cols + h * 256, 256), 256)
            keep = mask_ref[pl.ds(pl.multiple_of(h * 256, 256), 256), :] != 0
            block = jnp.concatenate(
                [rx2[:, n, 2 * h + i].reshape(S * 16, 128) for i in range(2)], axis=1
            )
            local = dot(block, fx_ref[...], ((0,), (0,)))
            for part in range(2):
                lanes = pl.ds(part * length, length)
                value = local[:, part * length : (part + 1) * length] + extra[rows, lanes]
                out_ref[rows, lanes] = jnp.where(keep, value, 0.0).astype(BF16)
            return c

        lax.fori_loop(0, G // 2, finish, 0)
        span = pl.ds(n * half_rows, half_rows)
        leave = pltpu.make_async_copy(out_ref.at[span], out_hbm.at[span], out_sem.at[n])
        leave.start()
        leaves.append(leave)

    dens_move.wait()
    for leave in leaves:
        leave.wait()


def hand_on(pieces, *refs):
    ins, outs, held = refs[:2], refs[2:4], refs[4:6]
    sem_in, sem_out = refs[6:]
    steps = []
    for i in range(2):
        rows = ins[i].shape[0] // pieces
        for k in range(pieces):
            span = pl.ds(k * rows, rows)
            here = held[i].at[span]
            steps.append(
                (
                    pltpu.make_async_copy(ins[i].at[span], here, sem_in.at[i, k]),
                    pltpu.make_async_copy(here, outs[i].at[span], sem_out.at[i, k]),
                )
            )
    for read, _ in steps:
        read.start()
    for read, write in steps:
        read.wait()
        write.start()
    for _, write in steps:
        write.wait()


def shards(
    orbitals,
    potential,
    cutoff_mask,
    channels,
    positions,
    proj_atom,
    proj_chan,
    coupling,
    occupations,
):
    N, rows_y, rows_z, wide = orbitals.shape
    length = wide // 2
    C = channels.shape[0]
    A = positions.shape[0]
    py, pz, bands = lax.axis_size("gy"), lax.axis_size("gz"), lax.axis_size("band")
    S = py * pz
    L = 2 * C * N * A
    G = rows_y * rows_z // 128
    cols = rows_y * rows_z
    ix, tz, t2, f2, tb, fx = [jnp.asarray(t) for t in tables(length, rows_z, pz)]
    hbm = pl.BlockSpec(memory_space=pl.ANY)
    smem = pl.BlockSpec(memory_space=pltpu.SMEM)
    sizes = (N, C, A, length, rows_y, rows_z, py, pz, bands)
    planes = (S, N, G, 16, 128)
    slim = (S, N, len(folds(length, rows_y)[0]), 16, 128)
    applied, density = pl.pallas_call(
        functools.partial(kernel, sizes),
        out_shape=(
            jax.ShapeDtypeStruct((N * cols, wide), BF16),
            jax.ShapeDtypeStruct(potential.shape, F32),
        ),
        in_specs=[smem] * 5 + [hbm] * 10,
        out_specs=(hbm, hbm),
        scratch_shapes=[
            pltpu.VMEM((N * cols, wide), BF16),
            pltpu.VMEM((cols, length), jnp.int32),
            pltpu.VMEM(ix.shape, BF16),
            pltpu.VMEM((C, cols, length), BF16),
            pltpu.VMEM(tz.shape, BF16),
            pltpu.VMEM(t2.shape, BF16),
            pltpu.VMEM(potential.shape, F32),
            pltpu.VMEM(f2.shape, BF16),
            pltpu.VMEM(tb.shape, BF16),
            pltpu.VMEM(fx.shape, BF16),
            pltpu.VMEM((N * cols, wide), BF16),
            pltpu.VMEM(potential.shape, F32),
            pltpu.SemaphoreType.DMA((N + 9,)),
            pltpu.SemaphoreType.DMA((N + 1,)),
            pltpu.VMEM((N * cols, wide), BF16),
            pltpu.VMEM(planes, BF16),
            pltpu.VMEM(planes, BF16),
            pltpu.VMEM(planes, BF16),
            pltpu.VMEM(planes, BF16),
            pltpu.VMEM(slim, BF16),
            pltpu.VMEM(slim, BF16),
            pltpu.VMEM(slim, BF16),
            pltpu.VMEM(slim, BF16),
            pltpu.VMEM((length * 16, length), F32),
            pltpu.VMEM(potential.shape, F32),
            pltpu.VMEM((bands,) + potential.shape, BF16),
            pltpu.VMEM((N * cols, wide), F32),
            pltpu.VMEM((2, cols, L), F32),
            pltpu.VMEM((L, C * N * wide), BF16),
            pltpu.VMEM((C * N * wide, L), BF16),
            pltpu.VMEM((256, C * N * wide), BF16),
            pltpu.VMEM((length * 4, length * 4), BF16),
            pltpu.VMEM((8, L), F32),
            pltpu.VMEM((S, 8, L), F32),
            pltpu.SemaphoreType.DMA((2, N, S)),
            pltpu.SemaphoreType.DMA((2, N, S)),
            pltpu.SemaphoreType.DMA((S,)),
            pltpu.SemaphoreType.DMA((S,)),
            pltpu.SemaphoreType.DMA((bands,)),
            pltpu.SemaphoreType.DMA((bands,)),
        ],
        compiler_params=pltpu.CompilerParams(
            collective_id=0, has_side_effects=True, vmem_limit_bytes=56 * 1024 * 1024
        ),
    )(
        positions.T,
        proj_atom,
        proj_chan,
        coupling,
        occupations,
        orbitals.reshape(N * cols, wide),
        cutoff_mask.reshape(cols, length),
        ix,
        channels.reshape(C, cols, length),
        tz,
        t2,
        potential,
        f2,
        tb,
        fx,
    )
    pieces = 4
    applied, density = pl.pallas_call(
        functools.partial(hand_on, pieces),
        out_shape=(
            jax.ShapeDtypeStruct((N * cols, wide), BF16),
            jax.ShapeDtypeStruct(potential.shape, F32),
        ),
        in_specs=[hbm] * 2,
        out_specs=(hbm, hbm),
        scratch_shapes=[
            pltpu.VMEM((N * cols, wide), BF16),
            pltpu.VMEM(potential.shape, F32),
            pltpu.SemaphoreType.DMA((2, pieces)),
            pltpu.SemaphoreType.DMA((2, pieces)),
        ],
    )(applied, density)
    return (applied.reshape(orbitals.shape), density)


def solution(mesh):
    placed = (
        P("band", "gy", "gz", None),
        P(("gy", "gz"), None, None),
        P("gy", "gz", None),
        P(None, "gy", "gz", None),
        P(),
        P(),
        P(),
        P(),
        P("band"),
    )
    return jax.shard_map(
        shards,
        mesh=mesh,
        in_specs=placed,
        out_specs=(P("band", "gy", "gz", None), P(("gy", "gz"), None, None)),
        check_vma=False,
    )
```
